256 devices in a mesh: dom: 64 (over z, x, core), tp: 4 (over y).
Axes of the slice: x: 4, y: 4, z: 8, core: 2. Of those that a mesh axis runs over, the one named last changes fastest.
Arguments:
- prefix_cache: bfloat16 [4, 2, 8192, 1024], P(None, None, 'dom', 'tp'), may hold values from -9 to 9
- suffix_cache: bfloat16 [128, 2, 512, 1024], P('dom', None, None, 'tp'), may hold values from -9 to 9
- queries: bfloat16 [128, 2, 8192], P('dom', None, 'tp'), may hold values from -170 to 170
- step_kv: bfloat16 [128, 2, 2, 1024], P('dom', None, None, 'tp'), may hold values from -9 to 9
- twist_weight: float32 [8192], P('tp'), may hold values from -0.24 to 0.24
- prior_weights: float32 [128], P('dom'), may hold values from -6 to 6
- prompt_ids: int32 [128], P('dom'), may hold values from 0 to 3, as said below
- ancestors: int32 [128], P('dom'), may hold values from 0 to 127, as said below
Outputs:
- log_weights: float32 [128], P('dom')
- copied_cache: bfloat16 [128, 2, 512, 1024], P('dom', None, None, 'tp')
- carried_kv: bfloat16 [128, 2, 1024], P('dom', None, 'tp')
- step_two_out: bfloat16 [128, 8192], P('dom', 'tp')
- twist_two: float32 [128], P('dom')
The draws below stay inside these ranges and needn't reach their ends.
Inputs may be any that keep to these rules, and one draw needn't show every extreme that they name: `prompt_ids`: prompt ids never fall along the particles; every prompt holds between 16 and 48 particles. `ancestors`: each slot's ancestor has the slot's prompt and lies at most 2 particles away from it; that distance is reached.
All inputs are finite; a program needn't handle non-finite values.
Results may differ from the reference program's by a relative error of at most 0.0075.
Values may be sent and summed in bfloat16 or wider, within the bound.
No kernel may reach another device: no remote copies, remote signals or barrier semaphores. Data moves between devices by JAX's collectives and lax.ppermute only.
A program may use at most 128 MiB of HBM per device.

```python
import math
import jax
import jax.numpy as jnp
from jax import lax

D = 8192
HEADS = 64
KV_HEADS = 8
HEAD_DIM = 128
PREFIX = 8192
SUF = 512
KVD = 1024
PARTICLES = 128
PROMPTS = 4
REACH = 2


def prompt_bounds(key):
    spacing = PARTICLES // PROMPTS
    jitter = jax.random.randint(key, (PROMPTS - 1,), -8, 9)
    return spacing * jnp.arange(1, PROMPTS, dtype=jnp.int32) + jitter.astype(jnp.int32)


def prompt_of(bounds):
    positions = jnp.arange(PARTICLES, dtype=jnp.int32)
    return jnp.sum((positions[:, None] >= bounds[None, :]).astype(jnp.int32), axis=1).astype(jnp.int32)


def draw_prompt_ids(key, part):
    bounds = prompt_bounds(key)
    return prompt_of(bounds)


def draw_ancestors(key, part):
    bounds = prompt_bounds(key)
    owners = prompt_of(bounds)
    key = jax.random.fold_in(key, 7)
    zero_row = jnp.zeros((1,), jnp.int32)
    last_row = jnp.full((1,), PARTICLES, jnp.int32)
    starts = jnp.concatenate([zero_row, bounds])[owners]
    ends = jnp.concatenate([bounds, last_row])[owners]
    offsets = jax.random.randint(key, (PARTICLES,), -REACH, REACH + 1).astype(jnp.int32)
    offsets = offsets.at[0].set(REACH)
    positions = jnp.arange(PARTICLES, dtype=jnp.int32)
    return jnp.clip(positions + offsets, starts, ends - 1).astype(jnp.int32)


def draw_queries(key, part):
    key = jax.random.fold_in(key, 3)
    values = 1.6 * jnp.clip(jax.random.normal(key, (PARTICLES, 2, HEADS, HEAD_DIM), jnp.float32), -6.0, 6.0)
    return values.reshape(PARTICLES, 2, D).astype(jnp.bfloat16)


def block_scale(stream_key, dims, cuts, smallest, largest):
    gain, own = 1.0, jax.random.fold_in(stream_key, 6)
    for position, parts in cuts:
        draws = jnp.exp(jax.random.uniform(jax.random.fold_in(own, position), (parts,), jnp.float32, smallest / len(cuts), largest / len(cuts)))
        gain = gain * jnp.repeat(draws, dims[position] // parts).reshape([-1 if axis == position else 1 for axis in range(len(dims))])
    return gain


def bell_draw(own_key, dims, scale, bound, shards=(), held_as=jnp.bfloat16):
    array = scale * jax.random.normal(own_key, dims, jnp.float32)
    if shards:
        array = array * block_scale(own_key, dims, shards, -0.22, 0.18)
    return jnp.clip(array, -bound, bound).astype(held_as)


def setup_inputs(seed: int = 0) -> dict:
    streams_of = jax.random.split(jax.random.key(seed), 9)
    prefix_cache = bell_draw(streams_of[0], (PROMPTS, 2, PREFIX, KVD), 1.5, 9.0, ((2, 64), (3, 4)))
    suffix_cache = bell_draw(streams_of[1], (PARTICLES, 2, SUF, KVD), 1.5, 9.0, ((0, 64), (3, 4)))
    queries = draw_queries(jax.random.fold_in(streams_of[8], 71), 0)
    step_kv = bell_draw(streams_of[3], (PARTICLES, 2, 2, KVD), 1.5, 9.0, ((0, 64), (3, 4)))
    twist_weight = bell_draw(streams_of[4], (D,), 0.04, 0.24, ((0, 4),), jnp.float32)
    prior_weights = bell_draw(streams_of[5], (PARTICLES,), 1.0, 6.0, ((0, 64),), jnp.float32)
    prompt_ids = draw_prompt_ids(jax.random.fold_in(streams_of[8], 71), 0)
    ancestors = draw_ancestors(jax.random.fold_in(streams_of[8], 71), 0)
    return {"prefix_cache": prefix_cache, "suffix_cache": suffix_cache, "queries": queries, "step_kv": step_kv, "twist_weight": twist_weight, "prior_weights": prior_weights, "prompt_ids": prompt_ids, "ancestors": ancestors}


def attend_part(queries_f, key_rows, value_rows):
    scores = jnp.einsum('scgd,tcd->scgt', queries_f, key_rows) / math.sqrt(HEAD_DIM)
    highest = lax.optimization_barrier(jnp.max(scores, axis=-1))
    shifted = jnp.exp(scores - highest[..., None])
    rounded = lax.optimization_barrier(shifted.astype(jnp.bfloat16)).astype(jnp.float32)
    weighted = jnp.einsum('scgt,tcd->scgd', rounded, value_rows)
    return (highest, weighted, lax.optimization_barrier(jnp.sum(shifted, axis=-1)))

def combine_parts(first_part, second_part):
    high_a, weighted_a, totals_a = first_part
    high_b, weighted_b, totals_b = second_part
    highest = jnp.maximum(high_a, high_b)
    scale_a = jnp.exp(high_a - highest)
    scale_b = jnp.exp(high_b - highest)
    upper = weighted_a * scale_a[..., None] + weighted_b * scale_b[..., None]
    lower = totals_a * scale_a + totals_b * scale_b
    return upper / lower[..., None]

def reference(prefix_cache, suffix_cache, queries, step_kv, twist_weight, prior_weights, prompt_ids, ancestors):
    group = HEADS // KV_HEADS
    indices = jnp.arange(PARTICLES, dtype=jnp.int32)

    def prefix_one(index):
        queries_f = queries[index].astype(jnp.float32).reshape(2, KV_HEADS, group, HEAD_DIM)
        prompt_rows = lax.dynamic_index_in_dim(prefix_cache, prompt_ids[index], 0, keepdims=False).astype(jnp.float32)
        key_rows = prompt_rows[0].reshape(PREFIX, KV_HEADS, HEAD_DIM)
        value_rows = prompt_rows[1].reshape(PREFIX, KV_HEADS, HEAD_DIM)
        return attend_part(queries_f, key_rows, value_rows)
    prefix_parts = lax.map(prefix_one, indices)

    def local_one(queries_row, key_rows, value_rows):
        queries_f = queries_row.astype(jnp.float32).reshape(1, KV_HEADS, group, HEAD_DIM)
        count = key_rows.shape[0]
        key_rows = key_rows.astype(jnp.float32).reshape(count, KV_HEADS, HEAD_DIM)
        value_rows = value_rows.astype(jnp.float32).reshape(count, KV_HEADS, HEAD_DIM)
        return attend_part(queries_f, key_rows, value_rows)

    def first_local(index):
        key_rows = jnp.concatenate([suffix_cache[index, 0], step_kv[index, 0, 0][None]], 0)
        value_rows = jnp.concatenate([suffix_cache[index, 1], step_kv[index, 0, 1][None]], 0)
        return local_one(queries[index, 0], key_rows, value_rows)
    first_parts = lax.map(first_local, indices)
    first_attn = combine_parts(tuple((piece[:, 0] for piece in prefix_parts)), tuple((piece[:, 0] for piece in first_parts)))
    first_attn = first_attn.reshape(PARTICLES, D)
    twist_one = lax.optimization_barrier(jnp.sum(first_attn * twist_weight, axis=-1))
    raised = prior_weights + twist_one
    table = prompt_ids[:, None] == jnp.arange(PROMPTS, dtype=jnp.int32)[None, :]
    prompt_top = lax.optimization_barrier(jnp.max(jnp.where(table, raised[:, None], -1e+30), axis=0))
    prompt_total = lax.optimization_barrier(jnp.sum(jnp.where(table, jnp.exp(raised[:, None] - prompt_top[None, :]), 0.0), axis=0))
    normalizer = jnp.log(prompt_total) + prompt_top
    log_weights = raised - lax.optimization_barrier(jnp.sum(jnp.where(table, normalizer[None, :], 0.0), axis=1))
    copied_cache = jnp.take(suffix_cache, ancestors, axis=0)
    carried_kv = jnp.take(step_kv[:, 0], ancestors, axis=0)

    def second_local(index):
        key_rows = jnp.concatenate([copied_cache[index, 0], carried_kv[index, 0][None], step_kv[index, 1, 0][None]], 0)
        value_rows = jnp.concatenate([copied_cache[index, 1], carried_kv[index, 1][None], step_kv[index, 1, 1][None]], 0)
        return local_one(queries[index, 1], key_rows, value_rows)
    second_parts = lax.map(second_local, indices)
    second_attn = combine_parts(tuple((piece[:, 1] for piece in prefix_parts)), tuple((piece[:, 0] for piece in second_parts)))
    second_attn = second_attn.reshape(PARTICLES, D)
    twist_two = lax.optimization_barrier(jnp.sum(second_attn * twist_weight, axis=-1))
    return (log_weights, copied_cache, carried_kv, second_attn.astype(jnp.bfloat16), twist_two)
```

```python
import math

import jax
import jax.numpy as jnp
from jax import lax
from jax.experimental import pallas as pl
from jax.experimental.pallas import tpu as pltpu
from jax.sharding import Mesh
from jax.sharding import PartitionSpec as P

HEAD_DIM = 128
PROMPTS = 4
GROUP = 8
NZ, NX, NC, NT = 8, 4, 2, 4
RING = NZ * NX
DOM = ("z", "x", "core")
WIDE = ("z", "x", "core", "tp")
FACTOR = 1.0 / math.sqrt(HEAD_DIM)
FACTOR2 = FACTOR * math.log2(math.e)
Q_ROWS = 64
ID_ROWS = 16
BLOCK_ROWS = Q_ROWS + ID_ROWS
OUT_ROWS = 32
TAIL_ROWS = 16
CHUNK = 8
F32 = jnp.float32
BF16 = jnp.bfloat16
NT_DIMS = (((1,), (1,)), ((), ()))
VMEM = pl.BlockSpec(memory_space=pltpu.VMEM)
SMEM = pl.BlockSpec(memory_space=pltpu.SMEM)
PARAMS = pltpu.CompilerParams(vmem_limit_bytes=48 * 1024 * 1024)


def lanes(shape):
    return lax.broadcasted_iota(jnp.int32, shape, len(shape) - 1)


def prep_kernel(ids_ref, q_ref, out_ref, rows_ref):
    for p in range(2):
        both = q_ref[p].astype(F32)
        for s in range(2):
            for h in range(16):
                kv, g = divmod(h, GROUP)
                row = kv * 32 + p * 16 + s * 8 + g
                rows_ref[row : row + 1, :] = both[s : s + 1, h * 128 : (h + 1) * 128]
    for p in range(2):
        start = Q_ROWS + p * 8
        rows_ref[start : start + 8, :] = jnp.broadcast_to(ids_ref[p].astype(F32), (8, 128))
    block = rows_ref[...].astype(BF16)
    for i in range(RING):
        out_ref[i] = block


def prefix_kernel(q_ref, own_ref, other_ref, w_ref, out_ref):
    keys, values = [], []
    for kv in range(2):
        cols = slice(kv * 128, (kv + 1) * 128)
        for kind, into in ((0, keys), (1, values)):
            into.append(
                jnp.concatenate(
                    [
                        jnp.concatenate([own_ref[g, kind, :, cols], other_ref[g, kind, :, cols]], axis=0)
                        for g in range(PROMPTS)
                    ],
                    axis=1,
                )
            )
    count = CHUNK * 32
    row_id = lax.broadcasted_iota(jnp.int32, (CHUNK, 32, 128), 1)
    lane_id = lanes((CHUNK, 32, 128))
    tail_row = lax.broadcasted_iota(jnp.int32, (CHUNK, TAIL_ROWS, 128), 1)
    for start in range(0, RING, CHUNK):
        ids = q_ref[start : start + CHUNK, Q_ROWS:BLOCK_ROWS, :].astype(F32)
        ids = ids.reshape(CHUNK, 2, 1, 8, 128)
        ids = jnp.broadcast_to(ids, (CHUNK, 2, 2, 8, 128)).reshape(count, 128)
        picks = [ids == float(g) for g in range(PROMPTS)]
        outs, tops0, tops1, dots = [], [], [], []
        for kv in range(2):
            q = q_ref[start : start + CHUNK, kv * 32 : (kv + 1) * 32, :].astype(F32).reshape(count, 128)
            spread = jnp.concatenate([jnp.where(pick, q, 0.0).astype(BF16) for pick in picks], axis=1)
            scores = lax.dot_general(spread, keys[kv], NT_DIMS, preferred_element_type=F32)
            top = jnp.max(scores, axis=1, keepdims=True)
            weights = jnp.exp2((scores - top) * FACTOR2)
            total = jnp.sum(weights, axis=1, keepdims=True)
            sums = jnp.dot(weights.astype(BF16), values[kv], preferred_element_type=F32)
            num = sums[:, 384:512]
            for g in (2, 1, 0):
                num = jnp.where(picks[g], sums[:, g * 128 : (g + 1) * 128], num)
            mean = (num / total).reshape(CHUNK, 2, 2, 8, 128)
            level = (top * FACTOR + jnp.log(total)).reshape(CHUNK, 2, 2, 8, 1)
            w = w_ref[kv * 8 : (kv + 1) * 8, :].reshape(1, 1, 8, 128)
            dots.append(jnp.sum(mean[:, :, 0] * w, axis=-1, keepdims=True))
            tops0.append(level[:, :, 0])
            tops1.append(level[:, :, 1])
            outs.append(mean[:, :, 1])

        def merge(pair):
            width = pair[0].shape[-1]
            return jnp.stack(pair, axis=2).reshape(CHUNK, 32, width)

        out_ref[start : start + CHUNK, 0:OUT_ROWS, :] = merge(outs).astype(BF16)
        packed = jnp.where(lane_id == row_id, merge(tops1), 0.0)
        packed = jnp.where(lane_id == row_id + 32, merge(tops0), packed)
        packed = jnp.where(lane_id == row_id + 64, merge(dots), packed)
        flat = jnp.sum(packed, axis=1)
        high = flat.astype(BF16).astype(F32)
        rest = flat - high
        mid = rest.astype(BF16).astype(F32)
        low = rest - mid
        tail = jnp.where(tail_row == 0, high[:, None, :], 0.0)
        tail = jnp.where(tail_row == 1, mid[:, None, :], tail)
        tail = jnp.where(tail_row == 2, low[:, None, :], tail)
        out_ref[start : start + CHUNK, OUT_ROWS:, :] = tail.astype(BF16)


def local_attend(q, keys, values, fresh):
    q16 = q.astype(BF16)
    scores = lax.dot_general(q16, keys, NT_DIMS, preferred_element_type=F32)
    extra = [jnp.sum(q * k, axis=1, keepdims=True) for k, _ in fresh]
    top = jnp.max(scores, axis=1, keepdims=True)
    for e in extra:
        top = jnp.maximum(top, e)
    weights = jnp.exp2((scores - top) * FACTOR2)
    total = jnp.sum(weights, axis=1, keepdims=True)
    num = jnp.dot(weights.astype(BF16), values, preferred_element_type=F32)
    for e, (_, v) in zip(extra, fresh):
        weight = jnp.exp2((e - top) * FACTOR2)
        total = total + weight
        num = num + weight.astype(BF16).astype(F32) * v
    return num / total, top * FACTOR + jnp.log(total)


def finish_kernel(
    anc_ref, ids_ref, prior_ref, q_ref, part_ref, own_ref, pair_ref, far_ref, kv_ref, pair_kv_ref, far_kv_ref,
    w_ref, copied_ref, carried_ref, out_ref, send_ref,
):
    core = lax.axis_index("core")
    base = ((lax.axis_index("z") * NX + lax.axis_index("x")) * NC + core) * 2 - 2
    for slot in range(2):
        pos = anc_ref[slot] - base
        side, which = pos // 2, pos % 2
        from_own = side == 1
        from_pair = side == jnp.where(core == 0, 2, 0)
        from_far = side == jnp.where(core == 0, 0, 2)
        for j in range(2):
            for flag, cache, kvs in (
                (from_own, own_ref, kv_ref),
                (from_pair, pair_ref, pair_kv_ref),
                (from_far, far_ref, far_kv_ref),
            ):

                @pl.when(flag & (which == j))
                def _():
                    copied_ref[slot] = cache[j]
                    carried_ref[slot] = kvs[j, 0:2]

    queries = q_ref[0].astype(F32)
    step_kv = kv_ref[...].astype(F32)
    carried = carried_ref[...].astype(F32)
    outs0, outs1, tops0, tops1 = [], [], [], []
    for p in range(2):
        for kv in range(2):
            cols = slice(kv * 128, (kv + 1) * 128)
            row = kv * 32 + p * 16
            k0, v0 = step_kv[p, 0:1, cols], step_kv[p, 1:2, cols]
            k1, v1 = step_kv[p, 2:3, cols], step_kv[p, 3:4, cols]
            kc, vc = carried[p, 0:1, cols], carried[p, 1:2, cols]
            mean, level = local_attend(
                queries[row : row + 8], own_ref[p, 0, :, cols], own_ref[p, 1, :, cols], [(k0, v0)]
            )
            outs0.append(mean)
            tops0.append(level)
            mean, level = local_attend(
                queries[row + 8 : row + 16],
                copied_ref[p, 0, :, cols],
                copied_ref[p, 1, :, cols],
                [(kc, vc), (k1, v1)],
            )
            outs1.append(mean)
            tops1.append(level)
    w = w_ref[...]
    w_rows = jnp.concatenate([w, w], axis=0)
    mine0 = jnp.concatenate(outs0, axis=0)
    mine1 = jnp.concatenate(outs1, axis=0)
    top0 = jnp.concatenate(tops0, axis=0)
    top1 = jnp.concatenate(tops1, axis=0)
    dot0 = jnp.sum(mine0 * w_rows, axis=1, keepdims=True)
    row_id = lax.broadcasted_iota(jnp.int32, (32, 128), 0)
    lane_id = lanes((32, 128))
    packed = jnp.where(lane_id == row_id, top1, 0.0)
    packed = jnp.where(lane_id == row_id + 32, top0, packed)
    packed = jnp.where(lane_id == row_id + 64, dot0, packed)
    mine = jnp.sum(packed, axis=0, keepdims=True)
    theirs = jnp.sum(part_ref[:, OUT_ROWS:, :].astype(F32), axis=1)
    top = jnp.maximum(jnp.max(theirs, axis=0, keepdims=True), mine)
    scale = jnp.exp(theirs - top)
    my_scale = jnp.exp(mine - top)
    inverse = 1.0 / (jnp.sum(scale, axis=0, keepdims=True) + my_scale)
    scale = scale * inverse
    my_scale = my_scale * inverse
    aligned = pltpu.roll(theirs, 96, 1)
    my_aligned = pltpu.roll(jnp.broadcast_to(mine, (8, 128)), 96, 1)[0:1]
    first = jnp.sum(scale * aligned, axis=0, keepdims=True) + my_scale * my_aligned
    one = lanes((1, 128))
    twist0 = [
        jnp.sum(jnp.where((one >= 32 + 16 * p) & (one < 48 + 16 * p), first, 0.0), axis=1, keepdims=True)
        for p in range(2)
    ]
    table = jnp.concatenate([scale, jnp.broadcast_to(my_scale, (96, 128))], axis=0).T
    attn = mine1 * table[0:32, 32:33]
    for i in range(RING):
        attn = attn + table[0:32, i : i + 1] * part_ref[i, 0:OUT_ROWS, :].astype(F32)
    weighted = jnp.sum(attn * w_rows, axis=1, keepdims=True)
    twist1 = [jnp.sum(weighted[p * 16 : (p + 1) * 16], axis=0, keepdims=True) for p in range(2)]
    for p in range(2):
        for h in range(16):
            out_ref[p : p + 1, h * 128 : (h + 1) * 128] = attn[p * 16 + h : p * 16 + h + 1, :]
    line = jnp.where(one == 0, twist0[0], 0.0)
    line = jnp.where(one == 1, twist0[1], line)
    line = jnp.where(one == 2, twist1[0], line)
    line = jnp.where(one == 3, twist1[1], line)
    for p in range(2):
        line = jnp.where(one == 4 + p, prior_ref[p], line)
        line = jnp.where(one == 6 + p, ids_ref[p].astype(F32), line)
    send_ref[...] = jnp.broadcast_to(line, send_ref.shape)


def weight_kernel(ids_ref, all_ref, log_ref, twist_ref):
    dom = (lax.axis_index("z") * NX + lax.axis_index("x")) * NC + lax.axis_index("core")
    rows = all_ref[...]
    count = rows.shape[0]
    total = rows + pltpu.roll(rows, count - 1, 0)
    total = total + pltpu.roll(total, count - 2, 0)
    raised = total + pltpu.roll(rows, 124, 1)
    ids = pltpu.roll(rows, 122, 1)
    row_id = lax.broadcasted_iota(jnp.int32, rows.shape, 0)
    lane_id = lanes(rows.shape)
    valid = (row_id % NT == 0) & (lane_id < 2)
    for p in range(2):
        member = valid & (ids == ids_ref[p].astype(F32))
        top = jnp.max(jnp.where(member, raised, -1e30), keepdims=True)
        amount = jnp.sum(jnp.where(member, jnp.exp(raised - top), 0.0), keepdims=True)
        mine = jnp.sum(jnp.where((row_id == dom * NT) & (lane_id == p), raised, 0.0), keepdims=True)
        twist = jnp.sum(jnp.where((row_id == dom * NT) & (lane_id == 2 + p), total, 0.0), keepdims=True)
        value = mine - (jnp.log(amount) + top)
        log_ref[p] = value[0, 0]
        twist_ref[p] = twist[0, 0]


def body(
    prefix_cache, suffix_cache, queries, step_kv, twist_weight, prior_weights, prompt_ids, ancestors
):
    swap = [(0, 1), (1, 0)]
    cross = [(i, i + 1) for i in range(1, NZ * NX * NC - 1, 2)]
    cross = cross + [(b, a) for a, b in cross]
    first_kv = step_kv[:, 0]
    other_prefix = lax.ppermute(prefix_cache, "core", swap)
    pair_cache = lax.ppermute(suffix_cache, "core", swap)
    far_cache = lax.ppermute(suffix_cache, DOM, cross)
    pair_kv = lax.ppermute(first_kv, "core", swap)
    far_kv = lax.ppermute(first_kv, DOM, cross)
    weight_rows = twist_weight.reshape(16, 128)

    blocks = pl.pallas_call(
        prep_kernel,
        out_shape=jax.ShapeDtypeStruct((RING, BLOCK_ROWS, 128), BF16),
        in_specs=[SMEM, VMEM],
        out_specs=VMEM,
        scratch_shapes=[pltpu.VMEM((BLOCK_ROWS, 128), F32)],
        compiler_params=PARAMS,
        name="prep",
    )(prompt_ids, queries)
    gathered = lax.all_to_all(blocks, ("z", "x"), 0, 0, tiled=True)
    parts = pl.pallas_call(
        prefix_kernel,
        out_shape=jax.ShapeDtypeStruct((RING, OUT_ROWS + TAIL_ROWS, 128), BF16),
        in_specs=[VMEM] * 4,
        out_specs=VMEM,
        compiler_params=PARAMS,
        name="prefix",
    )(gathered, prefix_cache, other_prefix, weight_rows)
    received = lax.all_to_all(parts, ("z", "x"), 0, 0, tiled=True)
    copied, carried, attn, line = pl.pallas_call(
        finish_kernel,
        out_shape=(
            jax.ShapeDtypeStruct(suffix_cache.shape, BF16),
            jax.ShapeDtypeStruct(first_kv.shape, BF16),
            jax.ShapeDtypeStruct((2, 2048), F32),
            jax.ShapeDtypeStruct((NZ * NX * NC * NT, 128), F32),
        ),
        in_specs=[SMEM] * 3 + [VMEM] * 9,
        out_specs=(VMEM,) * 4,
        compiler_params=PARAMS,
        name="finish",
    )(
        ancestors, prompt_ids, prior_weights, blocks[0:1], received, suffix_cache, pair_cache, far_cache,
        step_kv.reshape(2, 4, 256), pair_kv, far_kv, weight_rows,
    )
    lines = lax.all_to_all(line, WIDE, 0, 0, tiled=True)
    log_weights, twist_two = pl.pallas_call(
        weight_kernel,
        out_shape=(jax.ShapeDtypeStruct((2,), F32), jax.ShapeDtypeStruct((2,), F32)),
        in_specs=[SMEM, VMEM],
        out_specs=(SMEM, SMEM),
        compiler_params=PARAMS,
        name="weights",
    )(prompt_ids, lines)
    return (log_weights, copied, carried, attn.astype(BF16), twist_two)


def solution(mesh):
    inner = Mesh(mesh.devices.reshape(NZ, NX, NC, NT), WIDE)
    placed = (
        P(None, None, DOM, "tp"),
        P(DOM, None, None, "tp"),
        P(DOM, None, "tp"),
        P(DOM, None, None, "tp"),
        P("tp"),
        P(DOM),
        P(DOM),
        P(DOM),
    )
    return jax.shard_map(
        body,
        mesh=inner,
        in_specs=placed,
        out_specs=(
            P(DOM),
            P(DOM, None, None, "tp"),
            P(DOM, None, "tp"),
            P(DOM, "tp"),
            P(DOM),
        ),
        check_vma=False,
    )
```

```python
import math

import jax
import jax.numpy as jnp
from jax import lax
from jax.experimental import pallas as pl
from jax.experimental.pallas import tpu as pltpu
from jax.sharding import Mesh
from jax.sharding import PartitionSpec as P

HEAD_DIM = 128
PROMPTS = 4
GROUP = 8
NZ, NX, NC, NT = 8, 4, 2, 4
RING = NZ * NX
DOM = ("z", "x1", "x0", "core")
WIDE = ("z", "x1", "x0", "core", "tp")
PEERS = ("x0", "x1", "z")
FACTOR = 1.0 / math.sqrt(HEAD_DIM)
FACTOR2 = FACTOR * math.log2(math.e)
Q_ROWS = 64
ID_ROWS = 8
BLOCK_ROWS = Q_ROWS + ID_ROWS
OUT_ROWS = 32
PART_ROWS = OUT_ROWS + 40
CHUNK = 8
F32 = jnp.float32
BF16 = jnp.bfloat16
NT_DIMS = (((1,), (1,)), ((), ()))
VMEM = pl.BlockSpec(memory_space=pltpu.VMEM)
SMEM = pl.BlockSpec(memory_space=pltpu.SMEM)
LONG = pl.CostEstimate(flops=2 * 10**10, bytes_accessed=8 * 10**7, transcendentals=0)
PARAMS = pltpu.CompilerParams(vmem_limit_bytes=48 * 1024 * 1024)


def lanes(shape):
    return lax.broadcasted_iota(jnp.int32, shape, len(shape) - 1)


def ring_place():
    return (lax.axis_index("x0") * 2 + lax.axis_index("x1")) * NZ + lax.axis_index("z")


def prep_kernel(ids_ref, q_ref, out_ref, rows_ref):
    for p in range(2):
        both = q_ref[p].astype(F32)
        for s in range(2):
            for h in range(16):
                kv, g = divmod(h, GROUP)
                row = kv * 32 + p * 16 + s * 8 + g
                rows_ref[row : row + 1, :] = both[s : s + 1, h * 128 : (h + 1) * 128]
    first, second = ids_ref[0].astype(F32), ids_ref[1].astype(F32)
    rows_ref[Q_ROWS:BLOCK_ROWS, :] = jnp.where(lanes((ID_ROWS, 128)) < 64, first, second)
    block = rows_ref[...].astype(BF16)
    for i in range(RING):
        out_ref[i] = block


def prefix_kernel(ids_ref, prior_ref, q_ref, own_ref, other_ref, w_ref, level_ref, dot_ref, out_ref):
    keys, values = [], []
    for kv in range(2):
        cols = slice(kv * 128, (kv + 1) * 128)
        for kind, into in ((0, keys), (1, values)):
            into.append(
                jnp.concatenate(
                    [
                        jnp.concatenate([own_ref[g, kind, :, cols], other_ref[g, kind, :, cols]], axis=0)
                        for g in range(PROMPTS)
                    ],
                    axis=1,
                )
            )
    count = CHUNK * 32
    shape = (CHUNK, 32, 128)
    row_id = lax.broadcasted_iota(jnp.int32, shape, 1)
    lane_id = lanes(shape)
    spot = row_id + 32 * (lax.broadcasted_iota(jnp.int32, shape, 0) % 4)
    levels, dots, heads, bodies = [], [], [], []
    head_row = lax.broadcasted_iota(jnp.int32, (CHUNK, 8, 128), 1)
    place = ring_place()
    one = lanes((1, 128))
    prior = jnp.zeros((1, 128), F32)
    ids_row = jnp.zeros((1, 128), F32)
    for p in range(2):
        here = one // 16 == (place % 4) * 2 + p
        prior = jnp.where(here, prior_ref[p], prior)
        ids_row = jnp.where(here, ids_ref[p].astype(F32), ids_row)
    prior_parts = split(prior)
    for start in range(0, RING, CHUNK):
        block = q_ref[start : start + CHUNK].astype(F32)
        both = block[:, Q_ROWS:BLOCK_ROWS].reshape(CHUNK * ID_ROWS, 128)
        turned = pltpu.roll(both, 64, 1)
        left = lanes(both.shape) < 64
        ids = jnp.stack(
            [
                jnp.where(left, both, turned).reshape(CHUNK, 1, ID_ROWS, 128),
                jnp.where(left, turned, both).reshape(CHUNK, 1, ID_ROWS, 128),
            ],
            axis=1,
        )
        ids = jnp.broadcast_to(ids, (CHUNK, 2, 2, 8, 128)).reshape(count, 128)
        picks = [ids == float(g) for g in range(PROMPTS)]
        means, tops0, tops1, firsts = [], [], [], []
        for kv in range(2):
            q = block[:, kv * 32 : (kv + 1) * 32].reshape(count, 128)
            spread = jnp.concatenate([jnp.where(pick, q, 0.0).astype(BF16) for pick in picks], axis=1)
            scores = lax.dot_general(spread, keys[kv], NT_DIMS, preferred_element_type=F32)
            top = jnp.max(scores, axis=1, keepdims=True)
            weights = jnp.exp2((scores - top) * FACTOR2)
            total = jnp.sum(weights, axis=1, keepdims=True)
            sums = jnp.dot(weights.astype(BF16), values[kv], preferred_element_type=F32)
            num = sums[:, 384:512]
            for g in (2, 1, 0):
                num = jnp.where(picks[g], sums[:, g * 128 : (g + 1) * 128], num)
            mean = (num / total).reshape(CHUNK, 2, 2, 8, 128)
            level = (top * FACTOR + jnp.log(total)).reshape(CHUNK, 2, 2, 8, 1)
            w = w_ref[kv * 8 : (kv + 1) * 8, :].reshape(1, 1, 8, 128)
            firsts.append(jnp.sum(mean[:, :, 0] * w, axis=-1, keepdims=True))
            tops0.append(level[:, :, 0])
            tops1.append(level[:, :, 1])
            means.append(mean[:, :, 1])

        def merge(pair):
            return jnp.stack(pair, axis=2).reshape(CHUNK, 32, pair[0].shape[-1])

        def pack(pair):
            wide = jnp.where(lane_id == spot, merge(pair), 0.0)
            return jnp.sum(wide.reshape(CHUNK // 4, 128, 128), axis=1)

        bodies.append(merge(means))
        levels.append(pack(tops0))
        dots.append(pack(firsts))
        high, mid, low = split(jnp.sum(jnp.where(lane_id == row_id, merge(tops1), 0.0), axis=1))
        line = high + pltpu.roll(mid, 32, 1) + pltpu.roll(low, 64, 1)
        head = jnp.where(head_row == 0, line[:, None, :], 0.0)
        for r, row in enumerate((*prior_parts, ids_row)):
            head = jnp.where(head_row == r + 1, row[None], head)
        heads.append(head)
    level, dot = jnp.concatenate(levels, axis=0), jnp.concatenate(dots, axis=0)
    top = jnp.maximum(level, level_ref[...])
    old, new = jnp.exp(level - top), jnp.exp(level_ref[...] - top)
    dot = (dot * old + dot_ref[...] * new) / (old + new)
    level = top + jnp.log(old + new)
    for start, mean, head in zip(range(0, RING, CHUNK), bodies, heads):
        common = jnp.broadcast_to(jnp.concatenate([*split(level), dot], axis=0)[None], (CHUNK, 32, 128))
        out_ref[start : start + CHUNK] = jnp.concatenate([mean, head, common], axis=1).astype(BF16)


def split(value):
    high = value.astype(BF16).astype(F32)
    rest = value - high
    mid = rest.astype(BF16).astype(F32)
    return high, mid, rest - mid


def local_attend(q, keys, values, fresh):
    q16 = q.astype(BF16)
    scores = lax.dot_general(q16, keys, NT_DIMS, preferred_element_type=F32)
    extra = [jnp.sum(q * k, axis=1, keepdims=True) for k, _ in fresh]
    top = jnp.max(scores, axis=1, keepdims=True)
    for e in extra:
        top = jnp.maximum(top, e)
    weights = jnp.exp2((scores - top) * FACTOR2)
    total = jnp.sum(weights, axis=1, keepdims=True)
    num = jnp.dot(weights.astype(BF16), values, preferred_element_type=F32)
    for e, (_, v) in zip(extra, fresh):
        weight = jnp.exp2((e - top) * FACTOR2)
        total = total + weight
        num = num + weight.astype(BF16).astype(F32) * v
    return num / total, top * FACTOR + jnp.log(total)


def first_kernel(q_ref, own_ref, kv_ref, w_ref, level_ref, dot_ref):
    queries = q_ref[0].astype(F32)
    step_kv = kv_ref[...].astype(F32)
    means, tops = [], []
    for p in range(2):
        for kv in range(2):
            cols = slice(kv * 128, (kv + 1) * 128)
            row = kv * 32 + p * 16
            mean, top = local_attend(
                queries[row : row + 8],
                own_ref[p, 0, :, cols],
                own_ref[p, 1, :, cols],
                [(step_kv[p, 0:1, cols], step_kv[p, 1:2, cols])],
            )
            means.append(mean)
            tops.append(top)
    w = w_ref[...]
    dot = jnp.sum(jnp.concatenate(means, axis=0) * jnp.concatenate([w, w], axis=0), axis=1, keepdims=True)
    top = jnp.concatenate(tops, axis=0)
    place = ring_place()
    spot = lax.broadcasted_iota(jnp.int32, (32, 128), 0) + 32 * (place % 4)
    lane_id = lanes((32, 128))
    level_row = jnp.sum(jnp.where(lane_id == spot, top, 0.0), axis=0, keepdims=True)
    dot_row = jnp.sum(jnp.where(lane_id == spot, dot, 0.0), axis=0, keepdims=True)
    here = (lax.broadcasted_iota(jnp.int32, (8, 128), 0) == place // 4) & (lanes((8, 128)) // 32 == place % 4)
    level_ref[...] = jnp.where(here, level_row, -1e30)
    dot_ref[...] = jnp.where(here, dot_row, 0.0)


def second_kernel(
    anc_ref, q_ref, own_ref, pair_ref, far_ref, kv_ref, pair_kv_ref, far_kv_ref,
    copied_ref, carried_ref, mean_ref, level_ref,
):
    core = lax.axis_index("core")
    base = lax.axis_index("z") * NX + lax.axis_index("x1") * 2 + lax.axis_index("x0")
    base = (base * NC + core) * 2 - 2
    for slot in range(2):
        pos = anc_ref[slot] - base
        side, which = pos // 2, pos % 2
        from_own = side == 1
        from_pair = side == jnp.where(core == 0, 2, 0)
        from_far = side == jnp.where(core == 0, 0, 2)
        for j in range(2):
            for flag, cache, kvs in (
                (from_own, own_ref, kv_ref),
                (from_pair, pair_ref, pair_kv_ref),
                (from_far, far_ref, far_kv_ref),
            ):

                @pl.when(flag & (which == j))
                def _():
                    copied_ref[slot] = cache[j]
                    carried_ref[slot] = kvs[j, 0:2]

    queries = q_ref[0].astype(F32)
    step_kv = kv_ref[...].astype(F32)
    carried = carried_ref[...].astype(F32)
    tops = []
    for p in range(2):
        for kv in range(2):
            cols = slice(kv * 128, (kv + 1) * 128)
            row = kv * 32 + p * 16 + 8
            mean, top = local_attend(
                queries[row : row + 8],
                copied_ref[p, 0, :, cols],
                copied_ref[p, 1, :, cols],
                [
                    (carried[p, 0:1, cols], carried[p, 1:2, cols]),
                    (step_kv[p, 2:3, cols], step_kv[p, 3:4, cols]),
                ],
            )
            mean_ref[p * 16 + kv * 8 : p * 16 + kv * 8 + 8, :] = mean
            tops.append(top)
    top = jnp.concatenate(tops, axis=0)
    row_id = lax.broadcasted_iota(jnp.int32, (32, 128), 0)
    row = jnp.sum(jnp.where(lanes((32, 128)) == row_id, top, 0.0), axis=0, keepdims=True)
    level_ref[...] = jnp.broadcast_to(row, (8, 128))


def finish_kernel(part_ref, mean_ref, level_ref, w_ref, out_ref, send_ref):
    parts = part_ref[...].astype(F32)
    heads = parts[:, OUT_ROWS : OUT_ROWS + 8]
    head_row = lax.broadcasted_iota(jnp.int32, heads.shape, 1)
    theirs = jnp.sum(jnp.where(head_row == 0, heads, 0.0), axis=1)
    theirs = theirs + pltpu.roll(theirs, 96, 1) + pltpu.roll(theirs, 64, 1)
    mine = level_ref[0:1, :]
    top = jnp.maximum(jnp.max(theirs, axis=0, keepdims=True), mine)
    scale = jnp.exp(theirs - top)
    my_scale = jnp.exp(mine - top)
    inverse = 1.0 / (jnp.sum(scale, axis=0, keepdims=True) + my_scale)
    table = jnp.concatenate([scale * inverse, jnp.broadcast_to(my_scale * inverse, (96, 128))], axis=0).T
    attn = mean_ref[...] * table[0:32, 32:33]
    for i in range(RING):
        attn = attn + table[0:32, i : i + 1] * parts[i, 0:OUT_ROWS]
    w = w_ref[...]
    weighted = jnp.sum(attn * jnp.concatenate([w, w], axis=0), axis=1, keepdims=True)
    for p in range(2):
        for h in range(16):
            out_ref[p : p + 1, h * 128 : (h + 1) * 128] = attn[p * 16 + h : p * 16 + h + 1, :]

    high, mid, low, dot = (parts[:, OUT_ROWS + 8 * t : OUT_ROWS + 8 * (t + 1)] for t in (1, 2, 3, 4))
    level = high + mid + low
    top = jnp.max(level, axis=0)
    scale = jnp.exp(level - top[None])
    twist = jnp.sum(scale * dot, axis=0) / jnp.sum(scale, axis=0)
    for shift in (8, 4, 2, 1):
        twist = twist + pltpu.roll(twist, 128 - shift, 1)
    facts = jnp.sum(heads.reshape(8, 4, 8, 128), axis=1)
    fact_row = lax.broadcasted_iota(jnp.int32, facts.shape, 1)
    prior = jnp.sum(jnp.where((fact_row >= 1) & (fact_row <= 3), facts, 0.0), axis=1)
    ids = jnp.sum(jnp.where(fact_row == 4, facts, 0.0), axis=1)
    kind = lanes((8, 128)) % 16
    line = jnp.where(kind == 0, twist, jnp.where(kind == 1, prior, jnp.where(kind == 2, ids, 0.0)))
    one = lanes((8, 128))
    second = jnp.zeros((8, 128), F32)
    for p in range(2):
        part = jnp.sum(weighted[p * 16 : (p + 1) * 16], axis=0, keepdims=True)
        second = jnp.where(one == p, part, second)
    block = jnp.concatenate([line, second], axis=0)
    for i in range(NC * NT):
        send_ref[i] = block


def weight_kernel(ids_ref, all_ref, log_ref, twist_ref):
    core = lax.axis_index("core")
    place = ring_place()
    kind = lanes((8, 128)) % 16
    raised, ids, seconds = [], [], []
    for c in range(NC):
        rows = [all_ref[c * NT + t] for t in range(NT)]
        total = rows[0] + rows[1] + rows[2] + rows[3]
        raised.append(total[0:8] + pltpu.roll(rows[0][0:8], 127, 1))
        ids.append(pltpu.roll(rows[0][0:8], 126, 1))
        seconds.append(total[8:16])
    own = jnp.where(core == 0, raised[0], raised[1])
    second = jnp.where(core == 0, seconds[0], seconds[1])
    row_id = lax.broadcasted_iota(jnp.int32, (8, 128), 0)
    lane_id = lanes((8, 128))
    for p in range(2):
        me = ids_ref[p].astype(F32)
        members = [(kind == 0) & (i == me) for i in ids]
        masked = [jnp.where(m, r, -1e30) for m, r in zip(members, raised)]
        top = jnp.max(jnp.maximum(masked[0], masked[1]), keepdims=True)
        shares = [jnp.where(m, jnp.exp(r - top), 0.0) for m, r in zip(members, raised)]
        amount = jnp.sum(shares[0] + shares[1], keepdims=True)
        here = (row_id == place // 4) & (lane_id == (place % 4) * 32 + p * 16)
        mine = jnp.sum(jnp.where(here, own, 0.0), keepdims=True)
        value = mine - (jnp.log(amount) + top)
        log_ref[p] = value[0, 0]
        twist = jnp.sum(jnp.where((row_id == 0) & (lane_id == p), second, 0.0), keepdims=True)
        twist_ref[p] = twist[0, 0]


def body(
    prefix_cache, suffix_cache, queries, step_kv, twist_weight, prior_weights, prompt_ids, ancestors
):
    swap = [(0, 1), (1, 0)]
    cross = [(i, i + 1) for i in range(1, NZ * NX * NC - 1, 2)]
    cross = cross + [(b, a) for a, b in cross]
    first_kv = step_kv[:, 0]
    other_prefix = lax.ppermute(prefix_cache, "core", swap)
    pair_cache = lax.ppermute(suffix_cache, "core", swap)
    far_cache = lax.ppermute(suffix_cache, DOM, cross)
    pair_kv = lax.ppermute(first_kv, "core", swap)
    far_kv = lax.ppermute(first_kv, DOM, cross)
    weight_rows = twist_weight.reshape(16, 128)

    blocks = pl.pallas_call(
        prep_kernel,
        out_shape=jax.ShapeDtypeStruct((RING, BLOCK_ROWS, 128), BF16),
        in_specs=[SMEM, VMEM],
        out_specs=VMEM,
        scratch_shapes=[pltpu.VMEM((BLOCK_ROWS, 128), F32)],
        compiler_params=PARAMS,
        name="prep",
    )(prompt_ids, queries)
    gathered = lax.all_to_all(blocks, PEERS, 0, 0, tiled=True)
    local_kv = step_kv.reshape(2, 4, 256)
    late = lax.optimization_barrier((ancestors, prior_weights, prompt_ids, gathered))
    ancestors, prior_weights, prompt_ids = late[:3]
    plane = jax.ShapeDtypeStruct((8, 128), F32)
    level, dot = pl.pallas_call(
        first_kernel,
        out_shape=(plane, plane),
        in_specs=[VMEM] * 4,
        out_specs=(VMEM, VMEM),
        compiler_params=PARAMS,
        name="first_local",
    )(blocks[0:1], suffix_cache, local_kv, weight_rows)
    parts = pl.pallas_call(
        prefix_kernel,
        out_shape=jax.ShapeDtypeStruct((RING, PART_ROWS, 128), BF16),
        in_specs=[SMEM] * 2 + [VMEM] * 6,
        out_specs=VMEM,
        compiler_params=PARAMS,
        name="prefix",
    )(prompt_ids, prior_weights, gathered, prefix_cache, other_prefix, weight_rows, level, dot)
    received = lax.all_to_all(parts, PEERS, 0, 0, tiled=True)
    copied, carried, mean, second_level = pl.pallas_call(
        second_kernel,
        out_shape=(
            jax.ShapeDtypeStruct(suffix_cache.shape, BF16),
            jax.ShapeDtypeStruct(first_kv.shape, BF16),
            jax.ShapeDtypeStruct((32, 128), F32),
            plane,
        ),
        in_specs=[SMEM] + [VMEM] * 7,
        out_specs=(VMEM,) * 4,
        compiler_params=PARAMS,
        cost_estimate=LONG,
        name="second_local",
    )(ancestors, blocks[0:1], suffix_cache, pair_cache, far_cache, local_kv, pair_kv, far_kv)
    attn, send = pl.pallas_call(
        finish_kernel,
        out_shape=(
            jax.ShapeDtypeStruct((2, 2048), F32),
            jax.ShapeDtypeStruct((NC * NT, 16, 128), F32),
        ),
        in_specs=[VMEM] * 4,
        out_specs=(VMEM,) * 2,
        compiler_params=PARAMS,
        name="finish",
    )(received, mean, second_level, weight_rows)
    lines = lax.all_to_all(send, ("core", "tp"), 0, 0, tiled=True)
    log_weights, twist_two = pl.pallas_call(
        weight_kernel,
        out_shape=(jax.ShapeDtypeStruct((2,), F32), jax.ShapeDtypeStruct((2,), F32)),
        in_specs=[SMEM, VMEM],
        out_specs=(SMEM, SMEM),
        compiler_params=PARAMS,
        name="weights",
    )(prompt_ids, lines)
    return (log_weights, copied, carried, attn.astype(BF16), twist_two)


def solution(mesh):
    inner = Mesh(mesh.devices.reshape(NZ, 2, 2, NC, NT), WIDE)
    placed = (
        P(None, None, DOM, "tp"),
        P(DOM, None, None, "tp"),
        P(DOM, None, "tp"),
        P(DOM, None, None, "tp"),
        P("tp"),
        P(DOM),
        P(DOM),
        P(DOM),
    )
    return jax.shard_map(
        body,
        mesh=inner,
        in_specs=placed,
        out_specs=(
            P(DOM),
            P(DOM, None, None, "tp"),
            P(DOM, None, "tp"),
            P(DOM, "tp"),
            P(DOM),
        ),
        check_vma=False,
    )
```

```python
import math

import jax
import jax.numpy as jnp
from jax import lax
from jax.experimental import pallas as pl
from jax.experimental.pallas import tpu as pltpu
from jax.sharding import Mesh
from jax.sharding import PartitionSpec as P

HEAD_DIM = 128
PROMPTS = 4
GROUP = 8
NZ, NX, NC, NT = 8, 4, 2, 4
RING = 16
PLANE = RING // 4
DOM = ("z2", "z1", "z0", "x1", "x0", "core")
WIDE = ("z2", "z1", "z0", "x1", "x0", "core", "tp")
SHARE = ("x0", "core")
PEERS = ("x1", "z2", "z1", "z0")
FACTOR = 1.0 / math.sqrt(HEAD_DIM)
FACTOR2 = FACTOR * math.log2(math.e)
Q_ROWS = 64
ID_ROWS = 8
BLOCK_ROWS = Q_ROWS + ID_ROWS
OUT_ROWS = 32
PART_ROWS = OUT_ROWS + 8 + 4 * PLANE
CHUNK = 8
F32 = jnp.float32
BF16 = jnp.bfloat16
NT_DIMS = (((1,), (1,)), ((), ()))
VMEM = pl.BlockSpec(memory_space=pltpu.VMEM)
SMEM = pl.BlockSpec(memory_space=pltpu.SMEM)
HBM = pl.BlockSpec(memory_space=pltpu.HBM)
LONG = pl.CostEstimate(flops=2 * 10**10, bytes_accessed=8 * 10**7, transcendentals=0)
PARAMS = pltpu.CompilerParams(vmem_limit_bytes=16 * 1024 * 1024)
WHOLE = pltpu.CompilerParams(vmem_limit_bytes=60 * 1024 * 1024)


def lanes(shape):
    return lax.broadcasted_iota(jnp.int32, shape, len(shape) - 1)


def ring_place():
    place = 0
    for axis in PEERS:
        place = place * 2 + lax.axis_index(axis)
    return place


def prep_kernel(ids_hbm, q_hbm, out_ref, own_ref, ids_ref, q_ref, rows_ref, sems):
    copies = [
        pltpu.make_async_copy(src, dst, sems.at[n])
        for n, (src, dst) in enumerate(((ids_hbm, ids_ref), (q_hbm, q_ref)))
    ]
    for copy in copies:
        copy.start()
    for copy in copies:
        copy.wait()
    for p in range(2):
        both = q_ref[p].astype(F32)
        for s in range(2):
            for h in range(16):
                kv, g = divmod(h, GROUP)
                row = kv * 32 + p * 16 + s * 8 + g
                rows_ref[row : row + 1, :] = both[s : s + 1, h * 128 : (h + 1) * 128]
    first, second = ids_ref[0].astype(F32), ids_ref[1].astype(F32)
    rows_ref[Q_ROWS:BLOCK_ROWS, :] = jnp.where(lanes((ID_ROWS, 128)) < 64, first, second)
    block = rows_ref[...].astype(BF16)
    for i in range(RING):
        out_ref[i] = block
    own_ref[...] = rows_ref[0:Q_ROWS, :]


def prefix_kernel(
    q_ref, own_hbm, pair_hbm, next_hbm, cross_hbm, facts_ref, w_ref, level_ref, dot_ref, out_ref, cache_ref, sems
):
    copies = [
        pltpu.make_async_copy(src, cache_ref.at[n], sems.at[n])
        for n, src in enumerate((own_hbm, pair_hbm, next_hbm, cross_hbm))
    ]
    for copy in copies:
        copy.start()
    for copy in copies:
        copy.wait()
    keys, values = [], []
    for kv in range(2):
        cols = slice(kv * 128, (kv + 1) * 128)
        for kind, into in ((0, keys), (1, values)):
            into.append(
                jnp.concatenate(
                    [
                        jnp.concatenate([cache_ref[n, g, kind, :, cols] for n in range(4)], axis=0)
                        for g in range(PROMPTS)
                    ],
                    axis=1,
                )
            )
    count = CHUNK * 32
    shape = (CHUNK, 32, 128)
    row_id = lax.broadcasted_iota(jnp.int32, shape, 1)
    lane_id = lanes(shape)
    spot = row_id + 32 * (lax.broadcasted_iota(jnp.int32, shape, 0) % 4)
    levels, dots, heads, bodies = [], [], [], []
    head_row = lax.broadcasted_iota(jnp.int32, (CHUNK, 8, 128), 1)
    facts = facts_ref[...][None]
    for start in range(0, RING, CHUNK):
        block = q_ref[start : start + CHUNK].astype(F32)
        both = block[:, Q_ROWS:BLOCK_ROWS].reshape(CHUNK * ID_ROWS, 128)
        turned = pltpu.roll(both, 64, 1)
        left = lanes(both.shape) < 64
        ids = jnp.stack(
            [
                jnp.where(left, both, turned).reshape(CHUNK, 1, ID_ROWS, 128),
                jnp.where(left, turned, both).reshape(CHUNK, 1, ID_ROWS, 128),
            ],
            axis=1,
        )
        ids = jnp.broadcast_to(ids, (CHUNK, 2, 2, 8, 128)).reshape(count, 128)
        picks = [ids == float(g) for g in range(PROMPTS)]
        means, tops0, tops1, firsts = [], [], [], []
        for kv in range(2):
            q = block[:, kv * 32 : (kv + 1) * 32].reshape(count, 128)
            spread = jnp.concatenate([jnp.where(pick, q, 0.0).astype(BF16) for pick in picks], axis=1)
            scores = lax.dot_general(spread, keys[kv], NT_DIMS, preferred_element_type=F32)
            top = jnp.max(scores, axis=1, keepdims=True)
            weights = jnp.exp2((scores - top) * FACTOR2)
            total = jnp.sum(weights, axis=1, keepdims=True)
            sums = jnp.dot(weights.astype(BF16), values[kv], preferred_element_type=F32)
            num = sums[:, 384:512]
            for g in (2, 1, 0):
                num = jnp.where(picks[g], sums[:, g * 128 : (g + 1) * 128], num)
            mean = (num / total).reshape(CHUNK, 2, 2, 8, 128)
            level = (top * FACTOR + jnp.log(total)).reshape(CHUNK, 2, 2, 8, 1)
            w = w_ref[kv * 8 : (kv + 1) * 8, :].reshape(1, 1, 8, 128)
            firsts.append(jnp.sum(mean[:, :, 0] * w, axis=-1, keepdims=True))
            tops0.append(level[:, :, 0])
            tops1.append(level[:, :, 1])
            means.append(mean[:, :, 1])

        def merge(pair):
            return jnp.stack(pair, axis=2).reshape(CHUNK, 32, pair[0].shape[-1])

        def pack(pair):
            wide = jnp.where(lane_id == spot, merge(pair), 0.0)
            return jnp.sum(wide.reshape(CHUNK // 4, 128, 128), axis=1)

        bodies.append(merge(means))
        levels.append(pack(tops0))
        dots.append(pack(firsts))
        high, mid, low = split(jnp.sum(jnp.where(lane_id == row_id, merge(tops1), 0.0), axis=1))
        line = high + pltpu.roll(mid, 32, 1) + pltpu.roll(low, 64, 1)
        head = jnp.where(head_row == 0, line[:, None, :], facts)
        heads.append(head)
    level, dot = jnp.concatenate(levels, axis=0), jnp.concatenate(dots, axis=0)
    top = jnp.maximum(level, level_ref[...])
    old, new = jnp.exp(level - top), jnp.exp(level_ref[...] - top)
    dot = (dot * old + dot_ref[...] * new) / (old + new)
    level = top + jnp.log(old + new)
    for start, mean, head in zip(range(0, RING, CHUNK), bodies, heads):
        common = jnp.concatenate([*split(level), dot], axis=0)
        common = jnp.broadcast_to(common[None], (CHUNK, 4 * PLANE, 128))
        out_ref[start : start + CHUNK] = jnp.concatenate([mean, head, common], axis=1).astype(BF16)


def split(value):
    high = value.astype(BF16).astype(F32)
    rest = value - high
    mid = rest.astype(BF16).astype(F32)
    return high, mid, rest - mid


def local_attend(q, keys, values, fresh):
    q16 = q.astype(BF16)
    scores = lax.dot_general(q16, keys, NT_DIMS, preferred_element_type=F32)
    extra = [jnp.sum(q * k, axis=1, keepdims=True) for k, _ in fresh]
    top = jnp.max(scores, axis=1, keepdims=True)
    for e in extra:
        top = jnp.maximum(top, e)
    weights = jnp.exp2((scores - top) * FACTOR2)
    total = jnp.sum(weights, axis=1, keepdims=True)
    num = jnp.dot(weights.astype(BF16), values, preferred_element_type=F32)
    for e, (_, v) in zip(extra, fresh):
        weight = jnp.exp2((e - top) * FACTOR2)
        total = total + weight
        num = num + weight.astype(BF16).astype(F32) * v
    return num / total, top * FACTOR + jnp.log(total)


def first_kernel(ids_ref, prior_ref, q_ref, own_ref, kv_ref, w_ref, level_ref, dot_ref, facts_ref):
    queries = q_ref[...]
    step_kv = kv_ref[...].astype(F32)
    means, tops = [], []
    for p in range(2):
        for kv in range(2):
            cols = slice(kv * 128, (kv + 1) * 128)
            row = kv * 32 + p * 16
            mean, top = local_attend(
                queries[row : row + 8],
                own_ref[p, 0, :, cols],
                own_ref[p, 1, :, cols],
                [(step_kv[p, 0, 0:1, cols], step_kv[p, 0, 1:2, cols])],
            )
            means.append(mean)
            tops.append(top)
    w = w_ref[...]
    dot = jnp.sum(jnp.concatenate(means, axis=0) * jnp.concatenate([w, w], axis=0), axis=1, keepdims=True)
    top = jnp.concatenate(tops, axis=0)
    place = ring_place()
    spot = lax.broadcasted_iota(jnp.int32, (32, 128), 0) + 32 * (place % 4)
    lane_id = lanes((32, 128))
    level_row = jnp.sum(jnp.where(lane_id == spot, top, 0.0), axis=0, keepdims=True)
    dot_row = jnp.sum(jnp.where(lane_id == spot, dot, 0.0), axis=0, keepdims=True)
    here = lax.broadcasted_iota(jnp.int32, (PLANE, 128), 0) == place // 4
    here = here & (lanes((PLANE, 128)) // 32 == place % 4)
    level_ref[...] = jnp.where(here, level_row, -1e30)
    dot_ref[...] = jnp.where(here, dot_row, 0.0)
    slot = lanes((8, 128)) // 16 - (place % 4) * 2
    prior = jnp.where(slot == 0, prior_ref[0], jnp.where(slot == 1, prior_ref[1], 0.0))
    first, second = ids_ref[0].astype(F32), ids_ref[1].astype(F32)
    ids = jnp.where(slot == 0, first, jnp.where(slot == 1, second, 0.0))
    row_id = lax.broadcasted_iota(jnp.int32, (8, 128), 0)
    facts = jnp.where(row_id == 4, ids, 0.0)
    for r, part in enumerate(split(prior)):
        facts = jnp.where(row_id == r + 1, part, facts)
    facts_ref[...] = facts


def second_kernel(
    anc_hbm, q_ref, own_ref, pair_ref, far_ref, kv_ref, pair_kv_ref, far_kv_ref,
    copied_ref, carried_ref, mean_ref, level_ref, anc_ref, sem,
):
    copy = pltpu.make_async_copy(anc_hbm, anc_ref, sem)
    copy.start()
    copy.wait()
    core = lax.axis_index("core")
    base = 0
    for axis in DOM:
        base = base * 2 + lax.axis_index(axis)
    base = base * 2 - 2
    for slot in range(2):
        pos = anc_ref[slot] - base
        side, which = pos // 2, pos % 2
        from_own = side == 1
        from_pair = side == jnp.where(core == 0, 2, 0)
        from_far = side == jnp.where(core == 0, 0, 2)
        for j in range(2):
            for flag, cache, kvs in (
                (from_own, own_ref, kv_ref),
                (from_pair, pair_ref, pair_kv_ref),
                (from_far, far_ref, far_kv_ref),
            ):

                @pl.when(flag & (which == j))
                def _():
                    copied_ref[slot] = cache[j]
                    carried_ref[slot] = kvs[j, 0]

    queries = q_ref[...]
    step_kv = kv_ref[...].astype(F32)
    carried = carried_ref[...].astype(F32)
    tops = []
    for p in range(2):
        for kv in range(2):
            cols = slice(kv * 128, (kv + 1) * 128)
            row = kv * 32 + p * 16 + 8
            mean, top = local_attend(
                queries[row : row + 8],
                copied_ref[p, 0, :, cols],
                copied_ref[p, 1, :, cols],
                [
                    (carried[p, 0:1, cols], carried[p, 1:2, cols]),
                    (step_kv[p, 1, 0:1, cols], step_kv[p, 1, 1:2, cols]),
                ],
            )
            mean_ref[p * 16 + kv * 8 : p * 16 + kv * 8 + 8, :] = mean
            tops.append(top)
    top = jnp.concatenate(tops, axis=0)
    row_id = lax.broadcasted_iota(jnp.int32, (32, 128), 0)
    row = jnp.sum(jnp.where(lanes((32, 128)) == row_id, top, 0.0), axis=0, keepdims=True)
    level_ref[...] = jnp.broadcast_to(row, (8, 128))


def finish_kernel(part_ref, mean_ref, level_ref, w_ref, out_ref, send_ref, wide_ref):
    parts = part_ref[...].astype(F32)
    heads = parts[:, OUT_ROWS : OUT_ROWS + 8]
    head_row = lax.broadcasted_iota(jnp.int32, heads.shape, 1)
    theirs = jnp.sum(jnp.where(head_row == 0, heads, 0.0), axis=1)
    theirs = theirs + pltpu.roll(theirs, 96, 1) + pltpu.roll(theirs, 64, 1)
    mine = level_ref[0:1, :]
    top = jnp.maximum(jnp.max(theirs, axis=0, keepdims=True), mine)
    scale = jnp.exp(theirs - top)
    my_scale = jnp.exp(mine - top)
    inverse = 1.0 / (jnp.sum(scale, axis=0, keepdims=True) + my_scale)
    table = jnp.concatenate([scale * inverse, jnp.broadcast_to(my_scale * inverse, (128 - RING, 128))], axis=0).T
    attn = mean_ref[...] * table[0:32, RING : RING + 1]
    for i in range(RING):
        attn = attn + table[0:32, i : i + 1] * parts[i, 0:OUT_ROWS]
    w = w_ref[...]
    weighted = jnp.sum(attn * jnp.concatenate([w, w], axis=0), axis=1, keepdims=True)
    for p in range(2):
        for h in range(16):
            wide_ref[p : p + 1, h * 128 : (h + 1) * 128] = attn[p * 16 + h : p * 16 + h + 1, :]
    out_ref[...] = wide_ref[...].astype(BF16)

    base = OUT_ROWS + 8
    high, mid, low, dot = (parts[:, base + PLANE * t : base + PLANE * (t + 1)] for t in range(4))
    level = high + mid + low
    top = jnp.max(level, axis=0)
    scale = jnp.exp(level - top[None])
    twist = jnp.sum(scale * dot, axis=0) / jnp.sum(scale, axis=0)
    for shift in (8, 4, 2, 1):
        twist = twist + pltpu.roll(twist, 128 - shift, 1)
    facts = jnp.sum(heads.reshape(PLANE, 4, 8, 128), axis=1)
    fact_row = lax.broadcasted_iota(jnp.int32, facts.shape, 1)
    prior = jnp.sum(jnp.where((fact_row >= 1) & (fact_row <= 3), facts, 0.0), axis=1)
    ids = jnp.sum(jnp.where(fact_row == 4, facts, 0.0), axis=1)
    kind = lanes((PLANE, 128)) % 16
    line = jnp.where(kind == 0, twist, jnp.where(kind == 1, prior, jnp.where(kind == 2, ids, 0.0)))
    one = lanes((8 - PLANE, 128))
    second = jnp.zeros((8 - PLANE, 128), F32)
    for p in range(2):
        part = jnp.sum(weighted[p * 16 : (p + 1) * 16], axis=0, keepdims=True)
        second = jnp.where(one == p, part, second)
    block = jnp.concatenate([line, second], axis=0)
    for i in range(4 * NT):
        send_ref[i] = block


def weight_kernel(all_ref, log_ref, twist_ref):
    member = lax.axis_index("x0") * NC + lax.axis_index("core")
    place = ring_place()
    row_id = lax.broadcasted_iota(jnp.int32, (8, 128), 0)
    lane_id = lanes((8, 128))
    valid = (lane_id % 16 == 0) & (row_id < PLANE)
    raised, ids = [], []
    own = jnp.zeros((8, 128), F32)
    own_ids = jnp.zeros((8, 128), F32)
    for m in range(4):
        rows = [all_ref[m * NT + t] for t in range(NT)]
        total = rows[0] + rows[1] + rows[2] + rows[3]
        total = jnp.where(row_id < PLANE, total + pltpu.roll(rows[0], 127, 1), total)
        own = jnp.where(member == m, total, own)
        raised.append(total)
        ids.append(pltpu.roll(rows[0], 126, 1))
        own_ids = jnp.where(member == m, ids[-1], own_ids)
    for p in range(2):
        here = (row_id == place // 4) & (lane_id == (place % 4) * 32 + p * 16)
        me = jnp.sum(jnp.where(here, own_ids, 0.0), keepdims=True)
        members = [valid & (i == me) for i in ids]
        masked = [jnp.where(m, r, -1e30) for m, r in zip(members, raised)]
        top = jnp.maximum(jnp.maximum(masked[0], masked[1]), jnp.maximum(masked[2], masked[3]))
        top = jnp.max(top, keepdims=True)
        shares = [jnp.where(m, jnp.exp(r - top), 0.0) for m, r in zip(members, raised)]
        amount = jnp.sum(shares[0] + shares[1] + shares[2] + shares[3], keepdims=True)
        mine = jnp.sum(jnp.where(here, own, 0.0), keepdims=True)
        value = mine - (jnp.log(amount) + top)
        log_ref[p] = value[0, 0]
        twist = jnp.sum(jnp.where((row_id == PLANE) & (lane_id == p), own, 0.0), keepdims=True)
        twist_ref[p] = twist[0, 0]


def body(
    prefix_cache, suffix_cache, queries, step_kv, twist_weight, prior_weights, prompt_ids, ancestors
):
    swap = [(0, 1), (1, 0)]
    cross = [(i, i + 1) for i in range(1, NZ * NX * NC - 1, 2)]
    cross = cross + [(b, a) for a, b in cross]
    next_prefix = lax.ppermute(prefix_cache, "x0", swap)
    pair_prefix = lax.ppermute(prefix_cache, "core", swap)
    cross_prefix = lax.ppermute(next_prefix, "core", swap)
    weight_rows = twist_weight.reshape(16, 128)

    blocks, rows = pl.pallas_call(
        prep_kernel,
        out_shape=(
            jax.ShapeDtypeStruct((RING, BLOCK_ROWS, 128), BF16),
            jax.ShapeDtypeStruct((Q_ROWS, 128), F32),
        ),
        in_specs=[HBM] * 2,
        out_specs=(VMEM, VMEM),
        scratch_shapes=[
            pltpu.SMEM((2,), jnp.int32),
            pltpu.VMEM(queries.shape, BF16),
            pltpu.VMEM((BLOCK_ROWS, 128), F32),
            pltpu.SemaphoreType.DMA((2,)),
        ],
        compiler_params=WHOLE,
        name="prep",
    )(prompt_ids, queries)
    gathered = lax.all_to_all(blocks, PEERS, 0, 0, tiled=True)
    held = lax.optimization_barrier((suffix_cache, step_kv, blocks, prompt_ids, prior_weights))
    pair_cache = lax.ppermute(held[0], "core", swap)
    far_cache = lax.ppermute(held[0], DOM, cross)
    pair_kv = lax.ppermute(held[1], "core", swap)
    far_kv = lax.ppermute(held[1], DOM, cross)
    plane = jax.ShapeDtypeStruct((PLANE, 128), F32)
    level, dot, facts = pl.pallas_call(
        first_kernel,
        out_shape=(plane, plane, jax.ShapeDtypeStruct((8, 128), F32)),
        in_specs=[SMEM] * 2 + [VMEM] * 4,
        out_specs=(VMEM,) * 3,
        compiler_params=PARAMS,
        cost_estimate=LONG,
        name="first_local",
    )(held[3], held[4], rows, suffix_cache, step_kv, weight_rows)
    parts = pl.pallas_call(
        prefix_kernel,
        out_shape=jax.ShapeDtypeStruct((RING, PART_ROWS, 128), BF16),
        in_specs=[VMEM] + [HBM] * 4 + [VMEM] * 4,
        out_specs=VMEM,
        scratch_shapes=[
            pltpu.VMEM((4, *prefix_cache.shape), BF16),
            pltpu.SemaphoreType.DMA((4,)),
        ],
        compiler_params=WHOLE,
        name="prefix",
    )(
        gathered, prefix_cache, pair_prefix, next_prefix, cross_prefix, facts, weight_rows, level, dot
    )
    received = lax.all_to_all(parts, PEERS, 0, 0, tiled=True)
    copied, carried, mean, second_level = pl.pallas_call(
        second_kernel,
        out_shape=(
            jax.ShapeDtypeStruct(suffix_cache.shape, BF16),
            jax.ShapeDtypeStruct((2, 2, 256), BF16),
            jax.ShapeDtypeStruct((32, 128), F32),
            jax.ShapeDtypeStruct((8, 128), F32),
        ),
        in_specs=[HBM] + [VMEM] * 7,
        out_specs=(VMEM,) * 4,
        scratch_shapes=[pltpu.SMEM((2,), jnp.int32), pltpu.SemaphoreType.DMA],
        compiler_params=PARAMS,
        name="second_local",
    )(ancestors, rows, suffix_cache, pair_cache, far_cache, step_kv, pair_kv, far_kv)
    attn, send = pl.pallas_call(
        finish_kernel,
        out_shape=(
            jax.ShapeDtypeStruct((2, 2048), BF16),
            jax.ShapeDtypeStruct((4 * NT, 8, 128), F32),
        ),
        in_specs=[VMEM] * 4,
        out_specs=(VMEM,) * 2,
        scratch_shapes=[pltpu.VMEM((2, 2048), F32)],
        compiler_params=PARAMS,
        name="finish",
    )(received, mean, second_level, weight_rows)
    lines = lax.all_to_all(send, SHARE + ("tp",), 0, 0, tiled=True)
    log_weights, twist_two = pl.pallas_call(
        weight_kernel,
        out_shape=(jax.ShapeDtypeStruct((2,), F32), jax.ShapeDtypeStruct((2,), F32)),
        in_specs=[VMEM],
        out_specs=(SMEM, SMEM),
        compiler_params=PARAMS,
        name="weights",
    )(lines)
    return (log_weights, copied, carried, attn, twist_two)


def solution(mesh):
    inner = Mesh(mesh.devices.reshape(2, 2, 2, 2, 2, NC, NT), WIDE)
    placed = (
        P(None, None, DOM, "tp"),
        P(DOM, None, None, "tp"),
        P(DOM, None, "tp"),
        P(DOM, None, None, "tp"),
        P("tp"),
        P(DOM),
        P(DOM),
        P(DOM),
    )
    return jax.shard_map(
        body,
        mesh=inner,
        in_specs=placed,
        out_specs=(
            P(DOM),
            P(DOM, None, None, "tp"),
            P(DOM, None, "tp"),
            P(DOM, "tp"),
            P(DOM),
        ),
        check_vma=False,
    )
```

```python
import math

import jax
import jax.numpy as jnp
from jax import lax
from jax.experimental import pallas as pl
from jax.experimental.pallas import tpu as pltpu
from jax.sharding import Mesh
from jax.sharding import PartitionSpec as P

HEAD_DIM = 128
PROMPTS = 4
GROUP = 8
NZ, NX, NC, NT = 8, 4, 2, 4
RING = 16
PLANE = RING // 4
DOM = ("z2", "z1", "z0", "x1", "x0", "core")
WIDE = ("z2", "z1", "z0", "x1", "x0", "core", "tp")
SHARE = ("x0", "core")
PEERS = ("x1", "z2", "z1", "z0")
FACTOR = 1.0 / math.sqrt(HEAD_DIM)
FACTOR2 = FACTOR * math.log2(math.e)
Q_ROWS = 64
SUF = 512
TAIL = 16
ID_ROWS = 8
BLOCK_ROWS = Q_ROWS + ID_ROWS
OUT_ROWS = 32
PART_ROWS = OUT_ROWS + 8 + 4 * PLANE
CHUNK = 8
F32 = jnp.float32
BF16 = jnp.bfloat16
NT_DIMS = (((1,), (1,)), ((), ()))
VMEM = pl.BlockSpec(memory_space=pltpu.VMEM)
SMEM = pl.BlockSpec(memory_space=pltpu.SMEM)
HBM = pl.BlockSpec(memory_space=pltpu.HBM)
LONG = pl.CostEstimate(flops=2 * 10**10, bytes_accessed=8 * 10**7, transcendentals=0)
PARAMS = pltpu.CompilerParams(vmem_limit_bytes=16 * 1024 * 1024)
MOST = pltpu.CompilerParams(vmem_limit_bytes=52 * 1024 * 1024)
WHOLE = pltpu.CompilerParams(vmem_limit_bytes=60 * 1024 * 1024)


def lanes(shape):
    return lax.broadcasted_iota(jnp.int32, shape, len(shape) - 1)


def ring_place():
    place = 0
    for axis in PEERS:
        place = place * 2 + lax.axis_index(axis)
    return place


def prep_kernel(ids_hbm, q_hbm, out_ref, own_ref, ids_ref, q_ref, rows_ref, sems):
    copies = [
        pltpu.make_async_copy(src, dst, sems.at[n])
        for n, (src, dst) in enumerate(((ids_hbm, ids_ref), (q_hbm, q_ref)))
    ]
    for copy in copies:
        copy.start()
    for copy in copies:
        copy.wait()
    for p in range(2):
        both = q_ref[p].astype(F32)
        for s in range(2):
            for h in range(16):
                kv, g = divmod(h, GROUP)
                row = kv * 32 + p * 16 + s * 8 + g
                rows_ref[row : row + 1, :] = both[s : s + 1, h * 128 : (h + 1) * 128]
    first, second = ids_ref[0].astype(F32), ids_ref[1].astype(F32)
    rows_ref[Q_ROWS:BLOCK_ROWS, :] = jnp.where(lanes((ID_ROWS, 128)) < 64, first, second)
    block = rows_ref[...].astype(BF16)
    for i in range(RING):
        out_ref[i] = block
    own_ref[...] = rows_ref[0:Q_ROWS, :]


def prefix_kernel(q_ref, own_ref, pair_ref, next_ref, cross_ref, local_ref, w_ref, out_ref):
    caches = (own_ref, pair_ref, next_ref, cross_ref)

    def table(kind, kv):
        cols = slice(kv * 128, (kv + 1) * 128)
        return jnp.concatenate(
            [jnp.concatenate([cache[g, kind, :, cols] for cache in caches], axis=0) for g in range(PROMPTS)],
            axis=1,
        )

    count = CHUNK * 32
    shape = (CHUNK, 32, 128)
    row_id = lax.broadcasted_iota(jnp.int32, shape, 1)
    lane_id = lanes(shape)
    spot = row_id + 32 * (lax.broadcasted_iota(jnp.int32, shape, 0) % 4)
    levels, dots, heads, bodies = [], [], [], []
    head_row = lax.broadcasted_iota(jnp.int32, (CHUNK, 8, 128), 1)
    facts = local_ref[0:8, :][None]
    for start in range(0, RING, CHUNK):
        block = q_ref[start : start + CHUNK].astype(F32)
        both = block[:, Q_ROWS:BLOCK_ROWS].reshape(CHUNK * ID_ROWS, 128)
        turned = pltpu.roll(both, 64, 1)
        left = lanes(both.shape) < 64
        ids = jnp.stack(
            [
                jnp.where(left, both, turned).reshape(CHUNK, 1, ID_ROWS, 128),
                jnp.where(left, turned, both).reshape(CHUNK, 1, ID_ROWS, 128),
            ],
            axis=1,
        )
        ids = jnp.broadcast_to(ids, (CHUNK, 2, 2, 8, 128)).reshape(count, 128)
        picks = [ids == float(g) for g in range(PROMPTS)]
        means, tops0, tops1, firsts = [], [], [], []
        for kv in range(2):
            q = block[:, kv * 32 : (kv + 1) * 32].reshape(count, 128)
            spread = jnp.concatenate([jnp.where(pick, q, 0.0).astype(BF16) for pick in picks], axis=1)
            scores = lax.dot_general(spread, table(0, kv), NT_DIMS, preferred_element_type=F32)
            top = jnp.max(scores, axis=1, keepdims=True)
            weights = jnp.exp2((scores - top) * FACTOR2)
            total = jnp.sum(weights, axis=1, keepdims=True)
            sums = jnp.dot(weights.astype(BF16), table(1, kv), preferred_element_type=F32)
            num = sums[:, 384:512]
            for g in (2, 1, 0):
                num = jnp.where(picks[g], sums[:, g * 128 : (g + 1) * 128], num)
            mean = (num / total).reshape(CHUNK, 2, 2, 8, 128)
            level = (top * FACTOR + jnp.log(total)).reshape(CHUNK, 2, 2, 8, 1)
            w = w_ref[kv * 8 : (kv + 1) * 8, :].reshape(1, 1, 8, 128)
            firsts.append(jnp.sum(mean[:, :, 0] * w, axis=-1, keepdims=True))
            tops0.append(level[:, :, 0])
            tops1.append(level[:, :, 1])
            means.append(mean[:, :, 1])

        def merge(pair):
            return jnp.stack(pair, axis=2).reshape(CHUNK, 32, pair[0].shape[-1])

        def pack(pair):
            wide = jnp.where(lane_id == spot, merge(pair), 0.0)
            return jnp.sum(wide.reshape(CHUNK // 4, 128, 128), axis=1)

        bodies.append(merge(means))
        levels.append(pack(tops0))
        dots.append(pack(firsts))
        high, mid, low = split(jnp.sum(jnp.where(lane_id == row_id, merge(tops1), 0.0), axis=1))
        line = high + pltpu.roll(mid, 32, 1) + pltpu.roll(low, 64, 1)
        head = jnp.where(head_row == 0, line[:, None, :], facts)
        heads.append(head)
    level, dot = jnp.concatenate(levels, axis=0), jnp.concatenate(dots, axis=0)
    my_level, my_dot = local_ref[8 : 8 + PLANE, :], local_ref[8 + PLANE : 8 + 2 * PLANE, :]
    top = jnp.maximum(level, my_level)
    old, new = jnp.exp(level - top), jnp.exp(my_level - top)
    dot = (dot * old + my_dot * new) / (old + new)
    level = top + jnp.log(old + new)
    for start, mean, head in zip(range(0, RING, CHUNK), bodies, heads):
        common = jnp.concatenate([*split(level), dot], axis=0)
        common = jnp.broadcast_to(common[None], (CHUNK, 4 * PLANE, 128))
        out_ref[start : start + CHUNK] = jnp.concatenate([mean, head, common], axis=1).astype(BF16)


def split(value):
    high = value.astype(BF16).astype(F32)
    rest = value - high
    mid = rest.astype(BF16).astype(F32)
    return high, mid, rest - mid


def local_attend(q, keys, values, fresh):
    q16 = q.astype(BF16)
    scores = lax.dot_general(q16, keys, NT_DIMS, preferred_element_type=F32)
    extra = [jnp.sum(q * k, axis=1, keepdims=True) for k, _ in fresh]
    top = jnp.max(scores, axis=1, keepdims=True)
    for e in extra:
        top = jnp.maximum(top, e)
    weights = jnp.exp2((scores - top) * FACTOR2)
    total = jnp.sum(weights, axis=1, keepdims=True)
    num = jnp.dot(weights.astype(BF16), values, preferred_element_type=F32)
    for e, (_, v) in zip(extra, fresh):
        weight = jnp.exp2((e - top) * FACTOR2)
        total = total + weight
        num = num + weight.astype(BF16).astype(F32) * v
    return num / total, top * FACTOR + jnp.log(total)


def first_kernel(ids_ref, prior_ref, q_ref, kv_ref, w_ref, cache_hbm, out_ref, wide_hbm, wide_ref, sems):
    taken = pltpu.make_async_copy(cache_hbm, wide_ref.at[:, :, 0:SUF, :], sems.at[0])
    taken.start()
    queries = q_ref[...]
    step_kv = kv_ref[...].astype(F32)
    tail_row = lax.broadcasted_iota(jnp.int32, (TAIL, kv_ref.shape[-1]), 0)
    for p in range(2):
        for kind in range(2):
            line = step_kv[p, 0, kind : kind + 1, :]
            wide_ref[p, kind, SUF : SUF + TAIL, :] = jnp.where(tail_row == 0, line, 0.0).astype(BF16)
    taken.wait()
    given = pltpu.make_async_copy(wide_ref, wide_hbm, sems.at[1])
    given.start()
    means, tops = [], []
    for p in range(2):
        for kv in range(2):
            cols = slice(kv * 128, (kv + 1) * 128)
            row = kv * 32 + p * 16
            mean, top = local_attend(
                queries[row : row + 8],
                wide_ref[p, 0, 0:SUF, cols],
                wide_ref[p, 1, 0:SUF, cols],
                [(step_kv[p, 0, 0:1, cols], step_kv[p, 0, 1:2, cols])],
            )
            means.append(mean)
            tops.append(top)
    w = w_ref[...]
    dot = jnp.sum(jnp.concatenate(means, axis=0) * jnp.concatenate([w, w], axis=0), axis=1, keepdims=True)
    top = jnp.concatenate(tops, axis=0)
    place = ring_place()
    spot = lax.broadcasted_iota(jnp.int32, (32, 128), 0) + 32 * (place % 4)
    lane_id = lanes((32, 128))
    level_row = jnp.sum(jnp.where(lane_id == spot, top, 0.0), axis=0, keepdims=True)
    dot_row = jnp.sum(jnp.where(lane_id == spot, dot, 0.0), axis=0, keepdims=True)
    here = lax.broadcasted_iota(jnp.int32, (PLANE, 128), 0) == place // 4
    here = here & (lanes((PLANE, 128)) // 32 == place % 4)
    out_ref[8 : 8 + PLANE, :] = jnp.where(here, level_row, -1e30)
    out_ref[8 + PLANE : 8 + 2 * PLANE, :] = jnp.where(here, dot_row, 0.0)
    slot = lanes((8, 128)) // 16 - (place % 4) * 2
    prior = jnp.where(slot == 0, prior_ref[0], jnp.where(slot == 1, prior_ref[1], 0.0))
    first, second = ids_ref[0].astype(F32), ids_ref[1].astype(F32)
    ids = jnp.where(slot == 0, first, jnp.where(slot == 1, second, 0.0))
    row_id = lax.broadcasted_iota(jnp.int32, (8, 128), 0)
    facts = jnp.where(row_id == 4, ids, 0.0)
    for r, part in enumerate(split(prior)):
        facts = jnp.where(row_id == r + 1, part, facts)
    out_ref[0:8, :] = facts
    given.wait()


def second_kernel(
    anc_ref, q_ref, own_hbm, pair_hbm, far_hbm, kv_ref, copied_ref, carried_ref, mean_ref, wide_ref, sems
):
    core = lax.axis_index("core")
    base = 0
    for axis in DOM:
        base = base * 2 + lax.axis_index(axis)
    base = base * 2 - 2
    choices = []
    for slot in range(2):
        pos = anc_ref[slot] - base
        side, which = pos // 2, pos % 2
        from_own = side == 1
        from_pair = side == jnp.where(core == 0, 2, 0)
        from_far = side == jnp.where(core == 0, 0, 2)
        for j in range(2):
            for flag, cache in ((from_own, own_hbm), (from_pair, pair_hbm), (from_far, far_hbm)):
                copy = pltpu.make_async_copy(cache.at[j], wide_ref.at[slot], sems.at[slot])
                choices.append((flag & (which == j), copy))
    for flag, copy in choices:
        pl.when(flag)(copy.start)
    for flag, copy in choices:
        pl.when(flag)(copy.wait)
    for slot in range(2):
        copied_ref[slot] = wide_ref[slot, :, 0:SUF, :]
        for kind in range(2):
            tail = wide_ref[slot, kind, SUF : SUF + TAIL, :].astype(F32)
            carried_ref[slot, kind : kind + 1, :] = tail[0:1].astype(BF16)
    queries = q_ref[...]
    step_kv = kv_ref[...].astype(F32)
    carried = carried_ref[...].astype(F32)
    tops = []
    for p in range(2):
        for kv in range(2):
            cols = slice(kv * 128, (kv + 1) * 128)
            row = kv * 32 + p * 16 + 8
            mean, top = local_attend(
                queries[row : row + 8],
                wide_ref[p, 0, 0:SUF, cols],
                wide_ref[p, 1, 0:SUF, cols],
                [
                    (carried[p, 0:1, cols], carried[p, 1:2, cols]),
                    (step_kv[p, 1, 0:1, cols], step_kv[p, 1, 1:2, cols]),
                ],
            )
            mean_ref[p * 16 + kv * 8 : p * 16 + kv * 8 + 8, :] = mean
            tops.append(top)
    top = jnp.concatenate(tops, axis=0)
    row_id = lax.broadcasted_iota(jnp.int32, (32, 128), 0)
    row = jnp.sum(jnp.where(lanes((32, 128)) == row_id, top, 0.0), axis=0, keepdims=True)
    mean_ref[32:40, :] = jnp.broadcast_to(row, (8, 128))


def finish_kernel(part_ref, mean_ref, w_ref, out_ref, send_ref, wide_ref):
    parts = part_ref[...].astype(F32)
    heads = parts[:, OUT_ROWS : OUT_ROWS + 8]
    head_row = lax.broadcasted_iota(jnp.int32, heads.shape, 1)
    theirs = jnp.sum(jnp.where(head_row == 0, heads, 0.0), axis=1)
    theirs = theirs + pltpu.roll(theirs, 96, 1) + pltpu.roll(theirs, 64, 1)
    mine = mean_ref[32:33, :]
    top = jnp.maximum(jnp.max(theirs, axis=0, keepdims=True), mine)
    scale = jnp.exp(theirs - top)
    my_scale = jnp.exp(mine - top)
    inverse = 1.0 / (jnp.sum(scale, axis=0, keepdims=True) + my_scale)
    table = jnp.concatenate([scale * inverse, jnp.broadcast_to(my_scale * inverse, (128 - RING, 128))], axis=0).T
    attn = mean_ref[0:32, :] * table[0:32, RING : RING + 1]
    for i in range(RING):
        attn = attn + table[0:32, i : i + 1] * parts[i, 0:OUT_ROWS]
    w = w_ref[...]
    weighted = jnp.sum(attn * jnp.concatenate([w, w], axis=0), axis=1, keepdims=True)
    for p in range(2):
        for h in range(16):
            wide_ref[p : p + 1, h * 128 : (h + 1) * 128] = attn[p * 16 + h : p * 16 + h + 1, :]
    out_ref[...] = wide_ref[...].astype(BF16)

    base = OUT_ROWS + 8
    high, mid, low, dot = (parts[:, base + PLANE * t : base + PLANE * (t + 1)] for t in range(4))
    level = high + mid + low
    top = jnp.max(level, axis=0)
    scale = jnp.exp(level - top[None])
    twist = jnp.sum(scale * dot, axis=0) / jnp.sum(scale, axis=0)
    for shift in (8, 4, 2, 1):
        twist = twist + pltpu.roll(twist, 128 - shift, 1)
    facts = jnp.sum(heads.reshape(PLANE, 4, 8, 128), axis=1)
    fact_row = lax.broadcasted_iota(jnp.int32, facts.shape, 1)
    prior = jnp.sum(jnp.where((fact_row >= 1) & (fact_row <= 3), facts, 0.0), axis=1)
    ids = jnp.sum(jnp.where(fact_row == 4, facts, 0.0), axis=1)
    kind = lanes((PLANE, 128)) % 16
    line = jnp.where(kind == 0, twist, jnp.where(kind == 1, prior, jnp.where(kind == 2, ids, 0.0)))
    one = lanes((8 - PLANE, 128))
    second = jnp.zeros((8 - PLANE, 128), F32)
    for p in range(2):
        part = jnp.sum(weighted[p * 16 : (p + 1) * 16], axis=0, keepdims=True)
        second = jnp.where(one == p, part, second)
    block = jnp.concatenate([line, second], axis=0)
    for i in range(4 * NT):
        send_ref[i] = block


def weight_kernel(all_ref, log_ref, twist_ref):
    member = lax.axis_index("x0") * NC + lax.axis_index("core")
    place = ring_place()
    row_id = lax.broadcasted_iota(jnp.int32, (8, 128), 0)
    lane_id = lanes((8, 128))
    valid = (lane_id % 16 == 0) & (row_id < PLANE)
    raised, ids = [], []
    own = jnp.zeros((8, 128), F32)
    own_ids = jnp.zeros((8, 128), F32)
    for m in range(4):
        rows = [all_ref[m * NT + t] for t in range(NT)]
        total = rows[0] + rows[1] + rows[2] + rows[3]
        total = jnp.where(row_id < PLANE, total + pltpu.roll(rows[0], 127, 1), total)
        own = jnp.where(member == m, total, own)
        raised.append(total)
        ids.append(pltpu.roll(rows[0], 126, 1))
        own_ids = jnp.where(member == m, ids[-1], own_ids)
    for p in range(2):
        here = (row_id == place // 4) & (lane_id == (place % 4) * 32 + p * 16)
        me = jnp.sum(jnp.where(here, own_ids, 0.0), keepdims=True)
        members = [valid & (i == me) for i in ids]
        masked = [jnp.where(m, r, -1e30) for m, r in zip(members, raised)]
        top = jnp.maximum(jnp.maximum(masked[0], masked[1]), jnp.maximum(masked[2], masked[3]))
        top = jnp.max(top, keepdims=True)
        shares = [jnp.where(m, jnp.exp(r - top), 0.0) for m, r in zip(members, raised)]
        amount = jnp.sum(shares[0] + shares[1] + shares[2] + shares[3], keepdims=True)
        mine = jnp.sum(jnp.where(here, own, 0.0), keepdims=True)
        value = mine - (jnp.log(amount) + top)
        log_ref[p] = value[0, 0]
        twist = jnp.sum(jnp.where((row_id == PLANE) & (lane_id == p), own, 0.0), keepdims=True)
        twist_ref[p] = twist[0, 0]


def body(
    prefix_cache, suffix_cache, queries, step_kv, twist_weight, prior_weights, prompt_ids, ancestors
):
    swap = [(0, 1), (1, 0)]
    cross = [(i, i + 1) for i in range(1, NZ * NX * NC - 1, 2)]
    cross = cross + [(b, a) for a, b in cross]
    next_prefix = lax.ppermute(prefix_cache, "x0", swap)
    pair_prefix = lax.ppermute(prefix_cache, "core", swap)
    cross_prefix = lax.ppermute(next_prefix, "core", swap)
    weight_rows = twist_weight.reshape(16, 128)

    blocks, rows = pl.pallas_call(
        prep_kernel,
        out_shape=(
            jax.ShapeDtypeStruct((RING, BLOCK_ROWS, 128), BF16),
            jax.ShapeDtypeStruct((Q_ROWS, 128), F32),
        ),
        in_specs=[HBM] * 2,
        out_specs=(VMEM, VMEM),
        scratch_shapes=[
            pltpu.SMEM((2,), jnp.int32),
            pltpu.VMEM(queries.shape, BF16),
            pltpu.VMEM((BLOCK_ROWS, 128), F32),
            pltpu.SemaphoreType.DMA((2,)),
        ],
        compiler_params=WHOLE,
        name="prep",
    )(prompt_ids, queries)
    gathered = lax.all_to_all(blocks, PEERS, 0, 0, tiled=True)
    late_cache = lax.optimization_barrier((suffix_cache, blocks))[0]
    local, wide_cache = pl.pallas_call(
        first_kernel,
        out_shape=(
            jax.ShapeDtypeStruct((8 + 2 * PLANE, 128), F32),
            jax.ShapeDtypeStruct((2, 2, SUF + TAIL, 256), BF16),
        ),
        in_specs=[SMEM] * 2 + [VMEM] * 3 + [HBM],
        out_specs=(VMEM, HBM),
        scratch_shapes=[pltpu.VMEM((2, 2, SUF + TAIL, 256), BF16), pltpu.SemaphoreType.DMA((2,))],
        compiler_params=WHOLE,
        cost_estimate=LONG,
        name="first_local",
    )(prompt_ids, prior_weights, rows, step_kv, weight_rows, late_cache)
    held = lax.optimization_barrier((wide_cache, blocks))[0]
    pair_cache = lax.ppermute(held, "core", swap)
    far_cache = lax.ppermute(held, DOM, cross)
    parts = pl.pallas_call(
        prefix_kernel,
        out_shape=jax.ShapeDtypeStruct((RING, PART_ROWS, 128), BF16),
        in_specs=[VMEM] * 7,
        out_specs=VMEM,
        compiler_params=PARAMS,
        cost_estimate=LONG,
        name="prefix",
    )(
        gathered, prefix_cache, pair_prefix, next_prefix, cross_prefix, local, weight_rows
    )
    received = lax.all_to_all(parts, PEERS, 0, 0, tiled=True)
    copied, carried, mean = pl.pallas_call(
        second_kernel,
        out_shape=(
            jax.ShapeDtypeStruct(suffix_cache.shape, BF16),
            jax.ShapeDtypeStruct((2, 2, 256), BF16),
            jax.ShapeDtypeStruct((40, 128), F32),
        ),
        in_specs=[SMEM, VMEM] + [HBM] * 3 + [VMEM],
        out_specs=(VMEM,) * 3,
        scratch_shapes=[pltpu.VMEM((2, 2, SUF + TAIL, 256), BF16), pltpu.SemaphoreType.DMA((2,))],
        compiler_params=MOST,
        name="second_local",
    )(ancestors, rows, wide_cache, pair_cache, far_cache, step_kv)
    attn, send = pl.pallas_call(
        finish_kernel,
        out_shape=(
            jax.ShapeDtypeStruct((2, 2048), BF16),
            jax.ShapeDtypeStruct((4 * NT, 8, 128), F32),
        ),
        in_specs=[VMEM] * 3,
        out_specs=(VMEM,) * 2,
        scratch_shapes=[pltpu.VMEM((2, 2048), F32)],
        compiler_params=PARAMS,
        name="finish",
    )(received, mean, weight_rows)
    lines = lax.all_to_all(send, SHARE + ("tp",), 0, 0, tiled=True)
    log_weights, twist_two = pl.pallas_call(
        weight_kernel,
        out_shape=(jax.ShapeDtypeStruct((2,), F32), jax.ShapeDtypeStruct((2,), F32)),
        in_specs=[VMEM],
        out_specs=(SMEM, SMEM),
        compiler_params=PARAMS,
        name="weights",
    )(lines)
    return (log_weights, copied, carried, attn, twist_two)


def solution(mesh):
    inner = Mesh(mesh.devices.reshape(2, 2, 2, 2, 2, NC, NT), WIDE)
    placed = (
        P(None, None, DOM, "tp"),
        P(DOM, None, None, "tp"),
        P(DOM, None, "tp"),
        P(DOM, None, None, "tp"),
        P("tp"),
        P(DOM),
        P(DOM),
        P(DOM),
    )
    return jax.shard_map(
        body,
        mesh=inner,
        in_specs=placed,
        out_specs=(
            P(DOM),
            P(DOM, None, None, "tp"),
            P(DOM, None, "tp"),
            P(DOM, "tp"),
            P(DOM),
        ),
        check_vma=False,
    )
```

```python
import math

import jax
import jax.numpy as jnp
from jax import lax
from jax.experimental import pallas as pl
from jax.experimental.pallas import tpu as pltpu
from jax.sharding import Mesh
from jax.sharding import PartitionSpec as P

HEAD_DIM = 128
PROMPTS = 4
GROUP = 8
NZ, NX, NC, NT = 8, 4, 2, 4
RING = 16
PLANE = RING // 4
DOM = ("z2", "z1", "z0", "x1", "x0", "core")
WIDE = ("z2", "z1", "z0", "x1", "x0", "core", "tp")
SHARE = ("x0", "core")
PEERS = ("x1", "z2", "z1", "z0")
FACTOR = 1.0 / math.sqrt(HEAD_DIM)
FACTOR2 = FACTOR * math.log2(math.e)
Q_ROWS = 64
SUF = 512
TAIL = 16
ID_ROWS = 8
BLOCK_ROWS = Q_ROWS + ID_ROWS
OUT_ROWS = 32
PART_ROWS = OUT_ROWS + 8 + 4 * PLANE
CHUNK = 8
F32 = jnp.float32
BF16 = jnp.bfloat16
NT_DIMS = (((1,), (1,)), ((), ()))
VMEM = pl.BlockSpec(memory_space=pltpu.VMEM)
SMEM = pl.BlockSpec(memory_space=pltpu.SMEM)
HBM = pl.BlockSpec(memory_space=pltpu.HBM)
LONG = pl.CostEstimate(flops=2 * 10**10, bytes_accessed=8 * 10**7, transcendentals=0)
PARAMS = pltpu.CompilerParams(vmem_limit_bytes=16 * 1024 * 1024)
MOST = pltpu.CompilerParams(vmem_limit_bytes=52 * 1024 * 1024)
WHOLE = pltpu.CompilerParams(vmem_limit_bytes=60 * 1024 * 1024)


def lanes(shape):
    return lax.broadcasted_iota(jnp.int32, shape, len(shape) - 1)


def ring_place():
    place = 0
    for axis in PEERS:
        place = place * 2 + lax.axis_index(axis)
    return place


def prep_kernel(ids_hbm, q_hbm, out_ref, own_ref, ids_ref, q_ref, rows_ref, sems):
    copies = [
        pltpu.make_async_copy(src, dst, sems.at[n])
        for n, (src, dst) in enumerate(((ids_hbm, ids_ref), (q_hbm, q_ref)))
    ]
    for copy in copies:
        copy.start()
    for copy in copies:
        copy.wait()
    for p in range(2):
        both = q_ref[p].astype(F32)
        for s in range(2):
            for h in range(16):
                kv, g = divmod(h, GROUP)
                row = kv * 32 + p * 16 + s * 8 + g
                rows_ref[row : row + 1, :] = both[s : s + 1, h * 128 : (h + 1) * 128]
    first, second = ids_ref[0].astype(F32), ids_ref[1].astype(F32)
    rows_ref[Q_ROWS:BLOCK_ROWS, :] = jnp.where(lanes((ID_ROWS, 128)) < 64, first, second)
    block = rows_ref[...].astype(BF16)
    for i in range(RING):
        out_ref[i] = block
    own_ref[...] = rows_ref[0:Q_ROWS, :]


def prefix_kernel(q_ref, own_ref, pair_ref, next_ref, cross_ref, local_ref, w_ref, out_ref):
    caches = (own_ref, pair_ref, next_ref, cross_ref)

    def table(kind, kv):
        cols = slice(kv * 128, (kv + 1) * 128)
        return jnp.concatenate(
            [jnp.concatenate([cache[g, kind, :, cols] for cache in caches], axis=0) for g in range(PROMPTS)],
            axis=1,
        )

    count = CHUNK * 32
    shape = (CHUNK, 32, 128)
    row_id = lax.broadcasted_iota(jnp.int32, shape, 1)
    lane_id = lanes(shape)
    spot = row_id + 32 * (lax.broadcasted_iota(jnp.int32, shape, 0) % 4)
    levels, dots, heads, bodies = [], [], [], []
    head_row = lax.broadcasted_iota(jnp.int32, (CHUNK, 8, 128), 1)
    facts = local_ref[0:8, :][None]
    for start in range(0, RING, CHUNK):
        block = q_ref[start : start + CHUNK].astype(F32)
        both = block[:, Q_ROWS:BLOCK_ROWS].reshape(CHUNK * ID_ROWS, 128)
        turned = pltpu.roll(both, 64, 1)
        left = lanes(both.shape) < 64
        ids = jnp.stack(
            [
                jnp.where(left, both, turned).reshape(CHUNK, 1, ID_ROWS, 128),
                jnp.where(left, turned, both).reshape(CHUNK, 1, ID_ROWS, 128),
            ],
            axis=1,
        )
        ids = jnp.broadcast_to(ids, (CHUNK, 2, 2, 8, 128)).reshape(count, 128)
        picks = [ids == float(g) for g in range(PROMPTS)]
        means, tops0, tops1, firsts = [], [], [], []
        for kv in range(2):
            q = block[:, kv * 32 : (kv + 1) * 32].reshape(count, 128)
            spread = jnp.concatenate([jnp.where(pick, q, 0.0).astype(BF16) for pick in picks], axis=1)
            scores = lax.dot_general(spread, table(0, kv), NT_DIMS, preferred_element_type=F32)
            top = jnp.max(scores, axis=1, keepdims=True)
            weights = jnp.exp2((scores - top) * FACTOR2)
            total = jnp.sum(weights, axis=1, keepdims=True)
            sums = jnp.dot(weights.astype(BF16), table(1, kv), preferred_element_type=F32)
            num = sums[:, 384:512]
            for g in (2, 1, 0):
                num = jnp.where(picks[g], sums[:, g * 128 : (g + 1) * 128], num)
            mean = (num / total).reshape(CHUNK, 2, 2, 8, 128)
            level = (top * FACTOR + jnp.log(total)).reshape(CHUNK, 2, 2, 8, 1)
            w = w_ref[kv * 8 : (kv + 1) * 8, :].reshape(1, 1, 8, 128)
            firsts.append(jnp.sum(mean[:, :, 0] * w, axis=-1, keepdims=True))
            tops0.append(level[:, :, 0])
            tops1.append(level[:, :, 1])
            means.append(mean[:, :, 1])

        def merge(pair):
            return jnp.stack(pair, axis=2).reshape(CHUNK, 32, pair[0].shape[-1])

        def pack(pair):
            wide = jnp.where(lane_id == spot, merge(pair), 0.0)
            return jnp.sum(wide.reshape(CHUNK // 4, 128, 128), axis=1)

        bodies.append(merge(means))
        levels.append(pack(tops0))
        dots.append(pack(firsts))
        high, mid, low = split(jnp.sum(jnp.where(lane_id == row_id, merge(tops1), 0.0), axis=1))
        line = high + pltpu.roll(mid, 32, 1) + pltpu.roll(low, 64, 1)
        head = jnp.where(head_row == 0, line[:, None, :], facts)
        heads.append(head)
    level, dot = jnp.concatenate(levels, axis=0), jnp.concatenate(dots, axis=0)
    my_level, my_dot = local_ref[8 : 8 + PLANE, :], local_ref[8 + PLANE : 8 + 2 * PLANE, :]
    top = jnp.maximum(level, my_level)
    old, new = jnp.exp(level - top), jnp.exp(my_level - top)
    dot = (dot * old + my_dot * new) / (old + new)
    level = top + jnp.log(old + new)
    for start, mean, head in zip(range(0, RING, CHUNK), bodies, heads):
        common = jnp.concatenate([*split(level), dot], axis=0)
        common = jnp.broadcast_to(common[None], (CHUNK, 4 * PLANE, 128))
        out_ref[start : start + CHUNK] = jnp.concatenate([mean, head, common], axis=1).astype(BF16)


def split(value):
    high = value.astype(BF16).astype(F32)
    rest = value - high
    mid = rest.astype(BF16).astype(F32)
    return high, mid, rest - mid


def local_attend(q, keys, values, fresh):
    q16 = q.astype(BF16)
    scores = lax.dot_general(q16, keys, NT_DIMS, preferred_element_type=F32)
    extra = [jnp.sum(q * k, axis=1, keepdims=True) for k, _ in fresh]
    top = jnp.max(scores, axis=1, keepdims=True)
    for e in extra:
        top = jnp.maximum(top, e)
    weights = jnp.exp2((scores - top) * FACTOR2)
    total = jnp.sum(weights, axis=1, keepdims=True)
    num = jnp.dot(weights.astype(BF16), values, preferred_element_type=F32)
    for e, (_, v) in zip(extra, fresh):
        weight = jnp.exp2((e - top) * FACTOR2)
        total = total + weight
        num = num + weight.astype(BF16).astype(F32) * v
    return num / total, top * FACTOR + jnp.log(total)


def first_kernel(
    ids_hbm, prior_hbm, q_hbm, kv_hbm, w_hbm, cache_hbm, out_ref, wide_hbm,
    ids_ref, prior_ref, q_ref, kv_ref, w_ref, wide_ref, sems, in_sems, out_sems,
):
    taken = [
        pltpu.make_async_copy(cache_hbm.at[p], wide_ref.at[p, :, 0:SUF, :], in_sems.at[p]) for p in range(2)
    ]
    given = [pltpu.make_async_copy(wide_ref.at[p], wide_hbm.at[p], out_sems.at[p]) for p in range(2)]
    pairs = ((kv_hbm, kv_ref), (q_hbm, q_ref), (w_hbm, w_ref), (ids_hbm, ids_ref), (prior_hbm, prior_ref))
    small = [pltpu.make_async_copy(src, dst, sems.at[n]) for n, (src, dst) in enumerate(pairs)]
    taken[0].start()
    for copy in small:
        copy.start()
    taken[1].start()
    for copy in small:
        copy.wait()
    queries = q_ref[...]
    step_kv = kv_ref[...].astype(F32)
    tail_row = lax.broadcasted_iota(jnp.int32, (TAIL, kv_ref.shape[-1]), 0)
    for p in range(2):
        for kind in range(2):
            line = step_kv[p, 0, kind : kind + 1, :]
            wide_ref[p, kind, SUF : SUF + TAIL, :] = jnp.where(tail_row == 0, line, 0.0).astype(BF16)
    for p in range(2):
        taken[p].wait()
        given[p].start()
    means, tops = [], []
    for p in range(2):
        for kv in range(2):
            cols = slice(kv * 128, (kv + 1) * 128)
            row = kv * 32 + p * 16
            mean, top = local_attend(
                queries[row : row + 8],
                wide_ref[p, 0, 0:SUF, cols],
                wide_ref[p, 1, 0:SUF, cols],
                [(step_kv[p, 0, 0:1, cols], step_kv[p, 0, 1:2, cols])],
            )
            means.append(mean)
            tops.append(top)
    w = w_ref[...]
    dot = jnp.sum(jnp.concatenate(means, axis=0) * jnp.concatenate([w, w], axis=0), axis=1, keepdims=True)
    top = jnp.concatenate(tops, axis=0)
    place = ring_place()
    spot = lax.broadcasted_iota(jnp.int32, (32, 128), 0) + 32 * (place % 4)
    lane_id = lanes((32, 128))
    level_row = jnp.sum(jnp.where(lane_id == spot, top, 0.0), axis=0, keepdims=True)
    dot_row = jnp.sum(jnp.where(lane_id == spot, dot, 0.0), axis=0, keepdims=True)
    here = lax.broadcasted_iota(jnp.int32, (PLANE, 128), 0) == place // 4
    here = here & (lanes((PLANE, 128)) // 32 == place % 4)
    out_ref[8 : 8 + PLANE, :] = jnp.where(here, level_row, -1e30)
    out_ref[8 + PLANE : 8 + 2 * PLANE, :] = jnp.where(here, dot_row, 0.0)
    slot = lanes((8, 128)) // 16 - (place % 4) * 2
    prior = jnp.where(slot == 0, prior_ref[0], jnp.where(slot == 1, prior_ref[1], 0.0))
    first, second = ids_ref[0].astype(F32), ids_ref[1].astype(F32)
    ids = jnp.where(slot == 0, first, jnp.where(slot == 1, second, 0.0))
    row_id = lax.broadcasted_iota(jnp.int32, (8, 128), 0)
    facts = jnp.where(row_id == 4, ids, 0.0)
    for r, part in enumerate(split(prior)):
        facts = jnp.where(row_id == r + 1, part, facts)
    out_ref[0:8, :] = facts
    for copy in given:
        copy.wait()


def second_kernel(
    anc_ref, q_ref, own_hbm, pair_hbm, far_hbm, kv_ref, copied_hbm, carried_ref, mean_ref, wide_ref, sems, out_sems
):
    core = lax.axis_index("core")
    base = 0
    for axis in DOM:
        base = base * 2 + lax.axis_index(axis)
    base = base * 2 - 2
    choices = []
    for slot in range(2):
        pos = anc_ref[slot] - base
        side, which = pos // 2, pos % 2
        from_own = side == 1
        from_pair = side == jnp.where(core == 0, 2, 0)
        from_far = side == jnp.where(core == 0, 0, 2)
        for j in range(2):
            for flag, cache in ((from_own, own_hbm), (from_pair, pair_hbm), (from_far, far_hbm)):
                copy = pltpu.make_async_copy(cache.at[j], wide_ref.at[slot], sems.at[slot])
                choices.append((flag & (which == j), copy))
    for flag, copy in choices:
        pl.when(flag)(copy.start)
    for flag, copy in choices:
        pl.when(flag)(copy.wait)
    results = [
        pltpu.make_async_copy(wide_ref.at[slot, :, 0:SUF, :], copied_hbm.at[slot], out_sems.at[slot])
        for slot in range(2)
    ]
    for slot in range(2):
        results[slot].start()
        for kind in range(2):
            tail = wide_ref[slot, kind, SUF : SUF + TAIL, :].astype(F32)
            carried_ref[slot, kind : kind + 1, :] = tail[0:1].astype(BF16)
    queries = q_ref[...]
    step_kv = kv_ref[...].astype(F32)
    carried = carried_ref[...].astype(F32)
    tops = []
    for p in range(2):
        for kv in range(2):
            cols = slice(kv * 128, (kv + 1) * 128)
            row = kv * 32 + p * 16 + 8
            mean, top = local_attend(
                queries[row : row + 8],
                wide_ref[p, 0, 0:SUF, cols],
                wide_ref[p, 1, 0:SUF, cols],
                [
                    (carried[p, 0:1, cols], carried[p, 1:2, cols]),
                    (step_kv[p, 1, 0:1, cols], step_kv[p, 1, 1:2, cols]),
                ],
            )
            mean_ref[p * 16 + kv * 8 : p * 16 + kv * 8 + 8, :] = mean
            tops.append(top)
    top = jnp.concatenate(tops, axis=0)
    row_id = lax.broadcasted_iota(jnp.int32, (32, 128), 0)
    row = jnp.sum(jnp.where(lanes((32, 128)) == row_id, top, 0.0), axis=0, keepdims=True)
    mean_ref[32:40, :] = jnp.broadcast_to(row, (8, 128))
    for result in results:
        result.wait()


def finish_kernel(part_ref, mean_ref, w_ref, out_ref, send_ref, wide_ref):
    parts = part_ref[...].astype(F32)
    heads = parts[:, OUT_ROWS : OUT_ROWS + 8]
    head_row = lax.broadcasted_iota(jnp.int32, heads.shape, 1)
    theirs = jnp.sum(jnp.where(head_row == 0, heads, 0.0), axis=1)
    theirs = theirs + pltpu.roll(theirs, 96, 1) + pltpu.roll(theirs, 64, 1)
    mine = mean_ref[32:33, :]
    top = jnp.maximum(jnp.max(theirs, axis=0, keepdims=True), mine)
    scale = jnp.exp(theirs - top)
    my_scale = jnp.exp(mine - top)
    inverse = 1.0 / (jnp.sum(scale, axis=0, keepdims=True) + my_scale)
    table = jnp.concatenate([scale * inverse, jnp.broadcast_to(my_scale * inverse, (128 - RING, 128))], axis=0).T
    attn = mean_ref[0:32, :] * table[0:32, RING : RING + 1]
    for i in range(RING):
        attn = attn + table[0:32, i : i + 1] * parts[i, 0:OUT_ROWS]
    w = w_ref[...]
    weighted = jnp.sum(attn * jnp.concatenate([w, w], axis=0), axis=1, keepdims=True)
    for p in range(2):
        for h in range(16):
            wide_ref[p : p + 1, h * 128 : (h + 1) * 128] = attn[p * 16 + h : p * 16 + h + 1, :]
    out_ref[...] = wide_ref[...].astype(BF16)

    base = OUT_ROWS + 8
    high, mid, low, dot = (parts[:, base + PLANE * t : base + PLANE * (t + 1)] for t in range(4))
    level = high + mid + low
    top = jnp.max(level, axis=0)
    scale = jnp.exp(level - top[None])
    twist = jnp.sum(scale * dot, axis=0) / jnp.sum(scale, axis=0)
    for shift in (8, 4, 2, 1):
        twist = twist + pltpu.roll(twist, 128 - shift, 1)
    facts = jnp.sum(heads.reshape(PLANE, 4, 8, 128), axis=1)
    fact_row = lax.broadcasted_iota(jnp.int32, facts.shape, 1)
    prior = jnp.sum(jnp.where((fact_row >= 1) & (fact_row <= 3), facts, 0.0), axis=1)
    ids = jnp.sum(jnp.where(fact_row == 4, facts, 0.0), axis=1)
    kind = lanes((PLANE, 128)) % 16
    line = jnp.where(kind == 0, twist, jnp.where(kind == 1, prior, jnp.where(kind == 2, ids, 0.0)))
    one = lanes((8 - PLANE, 128))
    second = jnp.zeros((8 - PLANE, 128), F32)
    for p in range(2):
        part = jnp.sum(weighted[p * 16 : (p + 1) * 16], axis=0, keepdims=True)
        second = jnp.where(one == p, part, second)
    block = jnp.concatenate([line, second], axis=0)
    for i in range(4 * NT):
        send_ref[i] = block


def weight_kernel(all_ref, log_ref, twist_ref):
    member = lax.axis_index("x0") * NC + lax.axis_index("core")
    place = ring_place()
    row_id = lax.broadcasted_iota(jnp.int32, (8, 128), 0)
    lane_id = lanes((8, 128))
    valid = (lane_id % 16 == 0) & (row_id < PLANE)
    raised, ids = [], []
    own = jnp.zeros((8, 128), F32)
    own_ids = jnp.zeros((8, 128), F32)
    for m in range(4):
        rows = [all_ref[m * NT + t] for t in range(NT)]
        total = rows[0] + rows[1] + rows[2] + rows[3]
        total = jnp.where(row_id < PLANE, total + pltpu.roll(rows[0], 127, 1), total)
        own = jnp.where(member == m, total, own)
        raised.append(total)
        ids.append(pltpu.roll(rows[0], 126, 1))
        own_ids = jnp.where(member == m, ids[-1], own_ids)
    for p in range(2):
        here = (row_id == place // 4) & (lane_id == (place % 4) * 32 + p * 16)
        me = jnp.sum(jnp.where(here, own_ids, 0.0), keepdims=True)
        members = [valid & (i == me) for i in ids]
        masked = [jnp.where(m, r, -1e30) for m, r in zip(members, raised)]
        top = jnp.maximum(jnp.maximum(masked[0], masked[1]), jnp.maximum(masked[2], masked[3]))
        top = jnp.max(top, keepdims=True)
        shares = [jnp.where(m, jnp.exp(r - top), 0.0) for m, r in zip(members, raised)]
        amount = jnp.sum(shares[0] + shares[1] + shares[2] + shares[3], keepdims=True)
        mine = jnp.sum(jnp.where(here, own, 0.0), keepdims=True)
        value = mine - (jnp.log(amount) + top)
        log_ref[p] = value[0, 0]
        twist = jnp.sum(jnp.where((row_id == PLANE) & (lane_id == p), own, 0.0), keepdims=True)
        twist_ref[p] = twist[0, 0]


def body(
    prefix_cache, suffix_cache, queries, step_kv, twist_weight, prior_weights, prompt_ids, ancestors
):
    swap = [(0, 1), (1, 0)]
    cross = [(i, i + 1) for i in range(1, NZ * NX * NC - 1, 2)]
    cross = cross + [(b, a) for a, b in cross]
    next_prefix = lax.ppermute(prefix_cache, "x0", swap)
    pair_prefix = lax.ppermute(prefix_cache, "core", swap)
    weight_rows = twist_weight.reshape(16, 128)

    blocks, rows = pl.pallas_call(
        prep_kernel,
        out_shape=(
            jax.ShapeDtypeStruct((RING, BLOCK_ROWS, 128), BF16),
            jax.ShapeDtypeStruct((Q_ROWS, 128), F32),
        ),
        in_specs=[HBM] * 2,
        out_specs=(VMEM, VMEM),
        scratch_shapes=[
            pltpu.SMEM((2,), jnp.int32),
            pltpu.VMEM(queries.shape, BF16),
            pltpu.VMEM((BLOCK_ROWS, 128), F32),
            pltpu.SemaphoreType.DMA((2,)),
        ],
        compiler_params=WHOLE,
        name="prep",
    )(prompt_ids, queries)
    gathered = lax.all_to_all(blocks, PEERS, 0, 0, tiled=True)
    late_cache = lax.optimization_barrier((suffix_cache, blocks))[0]
    local, wide_cache = pl.pallas_call(
        first_kernel,
        out_shape=(
            jax.ShapeDtypeStruct((8 + 2 * PLANE, 128), F32),
            jax.ShapeDtypeStruct((2, 2, SUF + TAIL, 256), BF16),
        ),
        in_specs=[HBM] * 6,
        out_specs=(VMEM, HBM),
        scratch_shapes=[
            pltpu.SMEM((2,), jnp.int32),
            pltpu.SMEM((2,), F32),
            pltpu.VMEM((Q_ROWS, 128), F32),
            pltpu.VMEM(step_kv.shape, BF16),
            pltpu.VMEM((16, 128), F32),
            pltpu.VMEM((2, 2, SUF + TAIL, 256), BF16),
            pltpu.SemaphoreType.DMA((5,)),
            pltpu.SemaphoreType.DMA((2,)),
            pltpu.SemaphoreType.DMA((2,)),
        ],
        compiler_params=WHOLE,
        cost_estimate=LONG,
        name="first_local",
    )(prompt_ids, prior_weights, rows, step_kv, weight_rows, late_cache)
    held = lax.optimization_barrier((wide_cache, blocks))[0]
    after = lax.optimization_barrier((next_prefix, local))[0]
    cross_prefix = lax.ppermute(after, "core", swap)
    pair_cache = lax.ppermute(held, "core", swap)
    far_cache = lax.ppermute(held, DOM, cross)
    parts = pl.pallas_call(
        prefix_kernel,
        out_shape=jax.ShapeDtypeStruct((RING, PART_ROWS, 128), BF16),
        in_specs=[VMEM] * 7,
        out_specs=VMEM,
        compiler_params=PARAMS,
        cost_estimate=LONG,
        name="prefix",
    )(
        gathered, prefix_cache, pair_prefix, next_prefix, cross_prefix, local, weight_rows
    )
    received = lax.all_to_all(parts, PEERS, 0, 0, tiled=True)
    copied, carried, mean = pl.pallas_call(
        second_kernel,
        out_shape=(
            jax.ShapeDtypeStruct(suffix_cache.shape, BF16),
            jax.ShapeDtypeStruct((2, 2, 256), BF16),
            jax.ShapeDtypeStruct((40, 128), F32),
        ),
        in_specs=[SMEM, VMEM] + [HBM] * 3 + [VMEM],
        out_specs=(HBM, VMEM, VMEM),
        scratch_shapes=[
            pltpu.VMEM((2, 2, SUF + TAIL, 256), BF16),
            pltpu.SemaphoreType.DMA((2,)),
            pltpu.SemaphoreType.DMA((2,)),
        ],
        compiler_params=MOST,
        name="second_local",
    )(ancestors, rows, wide_cache, pair_cache, far_cache, step_kv)
    attn, send = pl.pallas_call(
        finish_kernel,
        out_shape=(
            jax.ShapeDtypeStruct((2, 2048), BF16),
            jax.ShapeDtypeStruct((4 * NT, 8, 128), F32),
        ),
        in_specs=[VMEM] * 3,
        out_specs=(VMEM,) * 2,
        scratch_shapes=[pltpu.VMEM((2, 2048), F32)],
        compiler_params=PARAMS,
        name="finish",
    )(received, mean, weight_rows)
    lines = lax.all_to_all(send, SHARE + ("tp",), 0, 0, tiled=True)
    log_weights, twist_two = pl.pallas_call(
        weight_kernel,
        out_shape=(jax.ShapeDtypeStruct((2,), F32), jax.ShapeDtypeStruct((2,), F32)),
        in_specs=[VMEM],
        out_specs=(SMEM, SMEM),
        compiler_params=PARAMS,
        name="weights",
    )(lines)
    return (log_weights, copied, carried, attn, twist_two)


def solution(mesh):
    inner = Mesh(mesh.devices.reshape(2, 2, 2, 2, 2, NC, NT), WIDE)
    placed = (
        P(None, None, DOM, "tp"),
        P(DOM, None, None, "tp"),
        P(DOM, None, "tp"),
        P(DOM, None, None, "tp"),
        P("tp"),
        P(DOM),
        P(DOM),
        P(DOM),
    )
    return jax.shard_map(
        body,
        mesh=inner,
        in_specs=placed,
        out_specs=(
            P(DOM),
            P(DOM, None, None, "tp"),
            P(DOM, None, "tp"),
            P(DOM, "tp"),
            P(DOM),
        ),
        check_vma=False,
    )
```

```python
import math

import jax
import jax.numpy as jnp
from jax import lax
from jax.experimental import pallas as pl
from jax.experimental.pallas import tpu as pltpu
from jax.sharding import Mesh
from jax.sharding import PartitionSpec as P

HEAD_DIM = 128
PROMPTS = 4
GROUP = 8
NZ, NX, NC, NT = 8, 4, 2, 4
RING = 16
PLANE = RING // 4
DOM = ("z2", "z1", "z0", "x1", "x0", "core")
WIDE = ("z2", "z1", "z0", "x1", "x0", "core", "tp")
SHARE = ("x0", "core")
PEERS = ("x1", "z2", "z1", "z0")
FACTOR = 1.0 / math.sqrt(HEAD_DIM)
FACTOR2 = FACTOR * math.log2(math.e)
Q_ROWS = 64
SUF = 512
TAIL = 16
ID_ROWS = 8
BLOCK_ROWS = Q_ROWS + ID_ROWS
OUT_ROWS = 32
PART_ROWS = OUT_ROWS + 8 + 4 * PLANE
CHUNK = 8
F32 = jnp.float32
BF16 = jnp.bfloat16
NT_DIMS = (((1,), (1,)), ((), ()))
VMEM = pl.BlockSpec(memory_space=pltpu.VMEM)
SMEM = pl.BlockSpec(memory_space=pltpu.SMEM)
HBM = pl.BlockSpec(memory_space=pltpu.HBM)
LONG = pl.CostEstimate(flops=2 * 10**10, bytes_accessed=8 * 10**7, transcendentals=0)
PARAMS = pltpu.CompilerParams(vmem_limit_bytes=16 * 1024 * 1024)
MOST = pltpu.CompilerParams(vmem_limit_bytes=52 * 1024 * 1024)
WHOLE = pltpu.CompilerParams(vmem_limit_bytes=60 * 1024 * 1024)


def lanes(shape):
    return lax.broadcasted_iota(jnp.int32, shape, len(shape) - 1)


def ring_place():
    place = 0
    for axis in PEERS:
        place = place * 2 + lax.axis_index(axis)
    return place


def prep_kernel(ids_hbm, q_hbm, out_ref, own_ref, ids_ref, q_ref, rows_ref, sems):
    copies = [
        pltpu.make_async_copy(src, dst, sems.at[n])
        for n, (src, dst) in enumerate(((ids_hbm, ids_ref), (q_hbm, q_ref)))
    ]
    for copy in copies:
        copy.start()
    for copy in copies:
        copy.wait()
    for p in range(2):
        both = q_ref[p].astype(F32)
        for s in range(2):
            for h in range(16):
                kv, g = divmod(h, GROUP)
                row = kv * 32 + p * 16 + s * 8 + g
                rows_ref[row : row + 1, :] = both[s : s + 1, h * 128 : (h + 1) * 128]
    first, second = ids_ref[0].astype(F32), ids_ref[1].astype(F32)
    rows_ref[Q_ROWS:BLOCK_ROWS, :] = jnp.where(lanes((ID_ROWS, 128)) < 64, first, second)
    block = rows_ref[...].astype(BF16)
    for i in range(RING):
        out_ref[i] = block
    own_ref[...] = rows_ref[0:Q_ROWS, :]


def prefix_kernel(q_ref, own_ref, pair_ref, next_ref, cross_ref, local_ref, w_ref, out_ref):
    caches = (own_ref, pair_ref, next_ref, cross_ref)

    def table(kind, kv):
        cols = slice(kv * 128, (kv + 1) * 128)
        return jnp.concatenate(
            [jnp.concatenate([cache[g, kind, :, cols] for cache in caches], axis=0) for g in range(PROMPTS)],
            axis=1,
        )

    count = CHUNK * 32
    shape = (CHUNK, 32, 128)
    row_id = lax.broadcasted_iota(jnp.int32, shape, 1)
    lane_id = lanes(shape)
    spot = row_id + 32 * (lax.broadcasted_iota(jnp.int32, shape, 0) % 4)
    levels, dots, heads, bodies = [], [], [], []
    head_row = lax.broadcasted_iota(jnp.int32, (CHUNK, 8, 128), 1)
    facts = local_ref[0:8, :][None]
    for start in range(0, RING, CHUNK):
        block = q_ref[start : start + CHUNK].astype(F32)
        both = block[:, Q_ROWS:BLOCK_ROWS].reshape(CHUNK * ID_ROWS, 128)
        turned = pltpu.roll(both, 64, 1)
        left = lanes(both.shape) < 64
        ids = jnp.stack(
            [
                jnp.where(left, both, turned).reshape(CHUNK, 1, ID_ROWS, 128),
                jnp.where(left, turned, both).reshape(CHUNK, 1, ID_ROWS, 128),
            ],
            axis=1,
        )
        ids = jnp.broadcast_to(ids, (CHUNK, 2, 2, 8, 128)).reshape(count, 128)
        picks = [ids == float(g) for g in range(PROMPTS)]
        means, tops0, tops1, firsts = [], [], [], []
        for kv in range(2):
            q = block[:, kv * 32 : (kv + 1) * 32].reshape(count, 128)
            spread = jnp.concatenate([jnp.where(pick, q, 0.0).astype(BF16) for pick in picks], axis=1)
            scores = lax.dot_general(spread, table(0, kv), NT_DIMS, preferred_element_type=F32)
            top = jnp.max(scores, axis=1, keepdims=True)
            weights = jnp.exp2((scores - top) * FACTOR2)
            total = jnp.sum(weights, axis=1, keepdims=True)
            sums = jnp.dot(weights.astype(BF16), table(1, kv), preferred_element_type=F32)
            num = sums[:, 384:512]
            for g in (2, 1, 0):
                num = jnp.where(picks[g], sums[:, g * 128 : (g + 1) * 128], num)
            mean = (num / total).reshape(CHUNK, 2, 2, 8, 128)
            level = (top * FACTOR + jnp.log(total)).reshape(CHUNK, 2, 2, 8, 1)
            w = w_ref[kv * 8 : (kv + 1) * 8, :].reshape(1, 1, 8, 128)
            firsts.append(jnp.sum(mean[:, :, 0] * w, axis=-1, keepdims=True))
            tops0.append(level[:, :, 0])
            tops1.append(level[:, :, 1])
            means.append(mean[:, :, 1])

        def merge(pair):
            return jnp.stack(pair, axis=2).reshape(CHUNK, 32, pair[0].shape[-1])

        def pack(pair):
            wide = jnp.where(lane_id == spot, merge(pair), 0.0)
            return jnp.sum(wide.reshape(CHUNK // 4, 128, 128), axis=1)

        bodies.append(merge(means))
        levels.append(pack(tops0))
        dots.append(pack(firsts))
        high, mid, low = split(jnp.sum(jnp.where(lane_id == row_id, merge(tops1), 0.0), axis=1))
        line = high + pltpu.roll(mid, 32, 1) + pltpu.roll(low, 64, 1)
        head = jnp.where(head_row == 0, line[:, None, :], facts)
        heads.append(head)
    level, dot = jnp.concatenate(levels, axis=0), jnp.concatenate(dots, axis=0)
    my_level, my_dot = local_ref[8 : 8 + PLANE, :], local_ref[8 + PLANE : 8 + 2 * PLANE, :]
    top = jnp.maximum(level, my_level)
    old, new = jnp.exp(level - top), jnp.exp(my_level - top)
    dot = (dot * old + my_dot * new) / (old + new)
    level = top + jnp.log(old + new)
    for start, mean, head in zip(range(0, RING, CHUNK), bodies, heads):
        common = jnp.concatenate([*split(level), dot], axis=0)
        common = jnp.broadcast_to(common[None], (CHUNK, 4 * PLANE, 128))
        out_ref[start : start + CHUNK] = jnp.concatenate([mean, head, common], axis=1).astype(BF16)


def split(value):
    high = value.astype(BF16).astype(F32)
    rest = value - high
    mid = rest.astype(BF16).astype(F32)
    return high, mid, rest - mid


def local_attend(q, keys, values, fresh):
    q16 = q.astype(BF16)
    scores = lax.dot_general(q16, keys, NT_DIMS, preferred_element_type=F32)
    extra = [jnp.sum(q * k, axis=1, keepdims=True) for k, _ in fresh]
    top = jnp.max(scores, axis=1, keepdims=True)
    for e in extra:
        top = jnp.maximum(top, e)
    weights = jnp.exp2((scores - top) * FACTOR2)
    total = jnp.sum(weights, axis=1, keepdims=True)
    num = jnp.dot(weights.astype(BF16), values, preferred_element_type=F32)
    for e, (_, v) in zip(extra, fresh):
        weight = jnp.exp2((e - top) * FACTOR2)
        total = total + weight
        num = num + weight.astype(BF16).astype(F32) * v
    return num / total, top * FACTOR + jnp.log(total)


def first_kernel(
    ids_hbm, prior_hbm, q_hbm, kv_hbm, w_hbm, cache_hbm, out_ref, wide_hbm,
    ids_ref, prior_ref, q_ref, kv_ref, w_ref, wide_ref, sems, in_sems, out_sems,
):
    taken = [
        pltpu.make_async_copy(cache_hbm.at[p], wide_ref.at[p, :, 0:SUF, :], in_sems.at[p]) for p in range(2)
    ]
    given = [pltpu.make_async_copy(wide_ref.at[p], wide_hbm.at[p], out_sems.at[p]) for p in range(2)]
    pairs = ((kv_hbm, kv_ref), (q_hbm, q_ref), (w_hbm, w_ref), (ids_hbm, ids_ref), (prior_hbm, prior_ref))
    small = [pltpu.make_async_copy(src, dst, sems.at[n]) for n, (src, dst) in enumerate(pairs)]
    taken[0].start()
    for copy in small:
        copy.start()
    taken[1].start()
    for copy in small:
        copy.wait()
    queries = q_ref[...]
    step_kv = kv_ref[...].astype(F32)
    tail_row = lax.broadcasted_iota(jnp.int32, (TAIL, kv_ref.shape[-1]), 0)
    for p in range(2):
        for kind in range(2):
            line = step_kv[p, 0, kind : kind + 1, :]
            wide_ref[p, kind, SUF : SUF + TAIL, :] = jnp.where(tail_row == 0, line, 0.0).astype(BF16)
    for p in range(2):
        taken[p].wait()
        given[p].start()
    means, tops = [], []
    for p in range(2):
        for kv in range(2):
            cols = slice(kv * 128, (kv + 1) * 128)
            row = kv * 32 + p * 16
            mean, top = local_attend(
                queries[row : row + 8],
                wide_ref[p, 0, 0:SUF, cols],
                wide_ref[p, 1, 0:SUF, cols],
                [(step_kv[p, 0, 0:1, cols], step_kv[p, 0, 1:2, cols])],
            )
            means.append(mean)
            tops.append(top)
    w = w_ref[...]
    dot = jnp.sum(jnp.concatenate(means, axis=0) * jnp.concatenate([w, w], axis=0), axis=1, keepdims=True)
    top = jnp.concatenate(tops, axis=0)
    place = ring_place()
    spot = lax.broadcasted_iota(jnp.int32, (32, 128), 0) + 32 * (place % 4)
    lane_id = lanes((32, 128))
    level_row = jnp.sum(jnp.where(lane_id == spot, top, 0.0), axis=0, keepdims=True)
    dot_row = jnp.sum(jnp.where(lane_id == spot, dot, 0.0), axis=0, keepdims=True)
    here = lax.broadcasted_iota(jnp.int32, (PLANE, 128), 0) == place // 4
    here = here & (lanes((PLANE, 128)) // 32 == place % 4)
    out_ref[8 : 8 + PLANE, :] = jnp.where(here, level_row, -1e30)
    out_ref[8 + PLANE : 8 + 2 * PLANE, :] = jnp.where(here, dot_row, 0.0)
    slot = lanes((8, 128)) // 16 - (place % 4) * 2
    prior = jnp.where(slot == 0, prior_ref[0], jnp.where(slot == 1, prior_ref[1], 0.0))
    first, second = ids_ref[0].astype(F32), ids_ref[1].astype(F32)
    ids = jnp.where(slot == 0, first, jnp.where(slot == 1, second, 0.0))
    row_id = lax.broadcasted_iota(jnp.int32, (8, 128), 0)
    facts = jnp.where(row_id == 4, ids, 0.0)
    for r, part in enumerate(split(prior)):
        facts = jnp.where(row_id == r + 1, part, facts)
    out_ref[0:8, :] = facts
    for copy in given:
        copy.wait()


def second_kernel(
    anc_ref, q_ref, own_hbm, pair_hbm, far_hbm, kv_ref, copied_hbm, carried_ref, mean_ref, wide_ref, sems, out_sems
):
    core = lax.axis_index("core")
    base = 0
    for axis in DOM:
        base = base * 2 + lax.axis_index(axis)
    base = base * 2 - 2
    choices = []
    for slot in range(2):
        pos = anc_ref[slot] - base
        side, which = pos // 2, pos % 2
        from_own = side == 1
        from_pair = side == jnp.where(core == 0, 2, 0)
        from_far = side == jnp.where(core == 0, 0, 2)
        for j in range(2):
            for flag, cache in ((from_own, own_hbm), (from_pair, pair_hbm), (from_far, far_hbm)):
                copy = pltpu.make_async_copy(cache.at[j], wide_ref.at[slot], sems.at[slot])
                choices.append((flag & (which == j), copy))
    for flag, copy in choices:
        pl.when(flag)(copy.start)
    for flag, copy in choices:
        pl.when(flag)(copy.wait)
    results = [
        pltpu.make_async_copy(wide_ref.at[slot, :, 0:SUF, :], copied_hbm.at[slot], out_sems.at[slot])
        for slot in range(2)
    ]
    for slot in range(2):
        results[slot].start()
        for kind in range(2):
            tail = wide_ref[slot, kind, SUF : SUF + TAIL, :].astype(F32)
            carried_ref[slot, kind : kind + 1, :] = tail[0:1].astype(BF16)
    queries = q_ref[...]
    step_kv = kv_ref[...].astype(F32)
    carried = carried_ref[...].astype(F32)
    tops = []
    for p in range(2):
        for kv in range(2):
            cols = slice(kv * 128, (kv + 1) * 128)
            row = kv * 32 + p * 16 + 8
            mean, top = local_attend(
                queries[row : row + 8],
                wide_ref[p, 0, 0:SUF, cols],
                wide_ref[p, 1, 0:SUF, cols],
                [
                    (carried[p, 0:1, cols], carried[p, 1:2, cols]),
                    (step_kv[p, 1, 0:1, cols], step_kv[p, 1, 1:2, cols]),
                ],
            )
            mean_ref[p * 16 + kv * 8 : p * 16 + kv * 8 + 8, :] = mean
            tops.append(top)
    top = jnp.concatenate(tops, axis=0)
    row_id = lax.broadcasted_iota(jnp.int32, (32, 128), 0)
    row = jnp.sum(jnp.where(lanes((32, 128)) == row_id, top, 0.0), axis=0, keepdims=True)
    mean_ref[32:40, :] = jnp.broadcast_to(row, (8, 128))
    for result in results:
        result.wait()


def finish_kernel(part_ref, mean_ref, w_ref, out_ref, send_ref, wide_ref):
    parts = part_ref[...].astype(F32)
    heads = parts[:, OUT_ROWS : OUT_ROWS + 8]
    head_row = lax.broadcasted_iota(jnp.int32, heads.shape, 1)
    theirs = jnp.sum(jnp.where(head_row == 0, heads, 0.0), axis=1)
    theirs = theirs + pltpu.roll(theirs, 96, 1) + pltpu.roll(theirs, 64, 1)
    mine = mean_ref[32:33, :]
    top = jnp.maximum(jnp.max(theirs, axis=0, keepdims=True), mine)
    scale = jnp.exp(theirs - top)
    my_scale = jnp.exp(mine - top)
    inverse = 1.0 / (jnp.sum(scale, axis=0, keepdims=True) + my_scale)
    table = jnp.concatenate([scale * inverse, jnp.broadcast_to(my_scale * inverse, (128 - RING, 128))], axis=0).T
    attn = mean_ref[0:32, :] * table[0:32, RING : RING + 1]
    for i in range(RING):
        attn = attn + table[0:32, i : i + 1] * parts[i, 0:OUT_ROWS]
    w = w_ref[...]
    weighted = jnp.sum(attn * jnp.concatenate([w, w], axis=0), axis=1, keepdims=True)
    for p in range(2):
        for h in range(16):
            wide_ref[p : p + 1, h * 128 : (h + 1) * 128] = attn[p * 16 + h : p * 16 + h + 1, :]
    out_ref[...] = wide_ref[...].astype(BF16)

    base = OUT_ROWS + 8
    high, mid, low, dot = (parts[:, base + PLANE * t : base + PLANE * (t + 1)] for t in range(4))
    level = high + mid + low
    top = jnp.max(level, axis=0)
    scale = jnp.exp(level - top[None])
    twist = jnp.sum(scale * dot, axis=0) / jnp.sum(scale, axis=0)
    for shift in (8, 4, 2, 1):
        twist = twist + pltpu.roll(twist, 128 - shift, 1)
    facts = jnp.sum(heads.reshape(PLANE, 4, 8, 128), axis=1)
    fact_row = lax.broadcasted_iota(jnp.int32, facts.shape, 1)
    prior = jnp.sum(jnp.where((fact_row >= 1) & (fact_row <= 3), facts, 0.0), axis=1)
    ids = jnp.sum(jnp.where(fact_row == 4, facts, 0.0), axis=1)
    kind = lanes((PLANE, 128)) % 16
    line = jnp.where(kind == 0, twist, jnp.where(kind == 1, prior, jnp.where(kind == 2, ids, 0.0)))
    one = lanes((8 - PLANE, 128))
    second = jnp.zeros((8 - PLANE, 128), F32)
    for p in range(2):
        part = jnp.sum(weighted[p * 16 : (p + 1) * 16], axis=0, keepdims=True)
        second = jnp.where(one == p, part, second)
    block = jnp.concatenate([line, second], axis=0)
    for i in range(4 * NT):
        send_ref[i] = block


def weight_kernel(all_ref, log_ref, twist_ref):
    member = lax.axis_index("x0") * NC + lax.axis_index("core")
    place = ring_place()
    row_id = lax.broadcasted_iota(jnp.int32, (8, 128), 0)
    lane_id = lanes((8, 128))
    valid = (lane_id % 16 == 0) & (row_id < PLANE)
    raised, ids = [], []
    own = jnp.zeros((8, 128), F32)
    own_ids = jnp.zeros((8, 128), F32)
    for m in range(4):
        rows = [all_ref[m * NT + t] for t in range(NT)]
        total = rows[0] + rows[1] + rows[2] + rows[3]
        total = jnp.where(row_id < PLANE, total + pltpu.roll(rows[0], 127, 1), total)
        own = jnp.where(member == m, total, own)
        raised.append(total)
        ids.append(pltpu.roll(rows[0], 126, 1))
        own_ids = jnp.where(member == m, ids[-1], own_ids)
    for p in range(2):
        here = (row_id == place // 4) & (lane_id == (place % 4) * 32 + p * 16)
        me = jnp.sum(jnp.where(here, own_ids, 0.0), keepdims=True)
        members = [valid & (i == me) for i in ids]
        masked = [jnp.where(m, r, -1e30) for m, r in zip(members, raised)]
        top = jnp.maximum(jnp.maximum(masked[0], masked[1]), jnp.maximum(masked[2], masked[3]))
        top = jnp.max(top, keepdims=True)
        shares = [jnp.where(m, jnp.exp(r - top), 0.0) for m, r in zip(members, raised)]
        amount = jnp.sum(shares[0] + shares[1] + shares[2] + shares[3], keepdims=True)
        mine = jnp.sum(jnp.where(here, own, 0.0), keepdims=True)
        value = mine - (jnp.log(amount) + top)
        log_ref[p] = value[0, 0]
        twist = jnp.sum(jnp.where((row_id == PLANE) & (lane_id == p), own, 0.0), keepdims=True)
        twist_ref[p] = twist[0, 0]


def body(
    prefix_cache, suffix_cache, queries, step_kv, twist_weight, prior_weights, prompt_ids, ancestors
):
    swap = [(0, 1), (1, 0)]
    cross = [(i, i + 1) for i in range(1, NZ * NX * NC - 1, 2)]
    cross = cross + [(b, a) for a, b in cross]
    next_prefix = lax.ppermute(prefix_cache, "x0", swap)
    pair_prefix = lax.ppermute(prefix_cache, "core", swap)
    weight_rows = twist_weight.reshape(16, 128)

    blocks, rows = pl.pallas_call(
        prep_kernel,
        out_shape=(
            jax.ShapeDtypeStruct((RING, BLOCK_ROWS, 128), BF16),
            jax.ShapeDtypeStruct((Q_ROWS, 128), F32),
        ),
        in_specs=[HBM] * 2,
        out_specs=(VMEM, VMEM),
        scratch_shapes=[
            pltpu.SMEM((2,), jnp.int32),
            pltpu.VMEM(queries.shape, BF16),
            pltpu.VMEM((BLOCK_ROWS, 128), F32),
            pltpu.SemaphoreType.DMA((2,)),
        ],
        compiler_params=WHOLE,
        name="prep",
    )(prompt_ids, queries)
    gathered = lax.all_to_all(blocks, PEERS, 0, 0, tiled=True)
    late_cache = lax.optimization_barrier((suffix_cache, blocks))[0]
    local, wide_cache = pl.pallas_call(
        first_kernel,
        out_shape=(
            jax.ShapeDtypeStruct((8 + 2 * PLANE, 128), F32),
            jax.ShapeDtypeStruct((2, 2, SUF + TAIL, 256), BF16),
        ),
        in_specs=[HBM] * 6,
        out_specs=(VMEM, HBM),
        scratch_shapes=[
            pltpu.SMEM((2,), jnp.int32),
            pltpu.SMEM((2,), F32),
            pltpu.VMEM((Q_ROWS, 128), F32),
            pltpu.VMEM(step_kv.shape, BF16),
            pltpu.VMEM((16, 128), F32),
            pltpu.VMEM((2, 2, SUF + TAIL, 256), BF16),
            pltpu.SemaphoreType.DMA((5,)),
            pltpu.SemaphoreType.DMA((2,)),
            pltpu.SemaphoreType.DMA((2,)),
        ],
        compiler_params=WHOLE,
        cost_estimate=LONG,
        name="first_local",
    )(prompt_ids, prior_weights, rows, step_kv, weight_rows, late_cache)
    held = lax.optimization_barrier((wide_cache, blocks))[0]
    after = lax.optimization_barrier((next_prefix, local))[0]
    cross_prefix = lax.ppermute(after, "core", swap)
    pair_cache = lax.ppermute(held, "core", swap)
    far_cache = lax.ppermute(held, DOM, cross)
    local = jnp.maximum(local, -3e38)
    parts = pl.pallas_call(
        prefix_kernel,
        out_shape=jax.ShapeDtypeStruct((RING, PART_ROWS, 128), BF16),
        in_specs=[VMEM] * 7,
        out_specs=VMEM,
        compiler_params=PARAMS,
        cost_estimate=LONG,
        name="prefix",
    )(
        gathered, prefix_cache, pair_prefix, next_prefix, cross_prefix, local, weight_rows
    )
    received = lax.all_to_all(parts, PEERS, 0, 0, tiled=True)
    copied, carried, mean = pl.pallas_call(
        second_kernel,
        out_shape=(
            jax.ShapeDtypeStruct(suffix_cache.shape, BF16),
            jax.ShapeDtypeStruct((2, 2, 256), BF16),
            jax.ShapeDtypeStruct((40, 128), F32),
        ),
        in_specs=[SMEM, VMEM] + [HBM] * 3 + [VMEM],
        out_specs=(HBM, VMEM, VMEM),
        scratch_shapes=[
            pltpu.VMEM((2, 2, SUF + TAIL, 256), BF16),
            pltpu.SemaphoreType.DMA((2,)),
            pltpu.SemaphoreType.DMA((2,)),
        ],
        compiler_params=MOST,
        name="second_local",
    )(ancestors, rows, wide_cache, pair_cache, far_cache, step_kv)
    attn, send = pl.pallas_call(
        finish_kernel,
        out_shape=(
            jax.ShapeDtypeStruct((2, 2048), BF16),
            jax.ShapeDtypeStruct((4 * NT, 8, 128), F32),
        ),
        in_specs=[VMEM] * 3,
        out_specs=(VMEM,) * 2,
        scratch_shapes=[pltpu.VMEM((2, 2048), F32)],
        compiler_params=PARAMS,
        name="finish",
    )(received, mean, weight_rows)
    lines = lax.all_to_all(send, SHARE + ("tp",), 0, 0, tiled=True)
    log_weights, twist_two = pl.pallas_call(
        weight_kernel,
        out_shape=(jax.ShapeDtypeStruct((2,), F32), jax.ShapeDtypeStruct((2,), F32)),
        in_specs=[VMEM],
        out_specs=(SMEM, SMEM),
        compiler_params=PARAMS,
        name="weights",
    )(lines)
    return (log_weights, copied, carried, attn, twist_two)


def solution(mesh):
    inner = Mesh(mesh.devices.reshape(2, 2, 2, 2, 2, NC, NT), WIDE)
    placed = (
        P(None, None, DOM, "tp"),
        P(DOM, None, None, "tp"),
        P(DOM, None, "tp"),
        P(DOM, None, None, "tp"),
        P("tp"),
        P(DOM),
        P(DOM),
        P(DOM),
    )
    return jax.shard_map(
        body,
        mesh=inner,
        in_specs=placed,
        out_specs=(
            P(DOM),
            P(DOM, None, None, "tp"),
            P(DOM, None, "tp"),
            P(DOM, "tp"),
            P(DOM),
        ),
        check_vma=False,
    )
```

```python
import math

import jax
import jax.numpy as jnp
from jax import lax
from jax.experimental import pallas as pl
from jax.experimental.pallas import tpu as pltpu
from jax.sharding import Mesh
from jax.sharding import PartitionSpec as P

HEAD_DIM = 128
PROMPTS = 4
GROUP = 8
NZ, NX, NC, NT = 8, 4, 2, 4
RING = 16
PLANE = RING // 4
DOM = ("z2", "z1", "z0", "x1", "x0", "core")
WIDE = ("z2", "z1", "z0", "x1", "x0", "core", "tp")
SHARE = ("x0", "core")
PEERS = ("x1", "z2", "z1", "z0")
FACTOR = 1.0 / math.sqrt(HEAD_DIM)
FACTOR2 = FACTOR * math.log2(math.e)
Q_ROWS = 64
SUF = 512
TAIL = 16
ID_ROWS = 8
BLOCK_ROWS = Q_ROWS + ID_ROWS
OUT_ROWS = 32
PART_ROWS = OUT_ROWS + 8 + 4 * PLANE
CHUNK = 8
F32 = jnp.float32
BF16 = jnp.bfloat16
NT_DIMS = (((1,), (1,)), ((), ()))
VMEM = pl.BlockSpec(memory_space=pltpu.VMEM)
SMEM = pl.BlockSpec(memory_space=pltpu.SMEM)
HBM = pl.BlockSpec(memory_space=pltpu.HBM)
LONG = pl.CostEstimate(flops=2 * 10**10, bytes_accessed=8 * 10**7, transcendentals=0)
PARAMS = pltpu.CompilerParams(vmem_limit_bytes=16 * 1024 * 1024)
MOST = pltpu.CompilerParams(vmem_limit_bytes=52 * 1024 * 1024)
WHOLE = pltpu.CompilerParams(vmem_limit_bytes=60 * 1024 * 1024)


def lanes(shape):
    return lax.broadcasted_iota(jnp.int32, shape, len(shape) - 1)


def ring_place():
    place = 0
    for axis in PEERS:
        place = place * 2 + lax.axis_index(axis)
    return place


def prep_kernel(ids_hbm, q_hbm, out_ref, own_ref, ids_ref, q_ref, rows_ref, sems):
    copies = [
        pltpu.make_async_copy(src, dst, sems.at[n])
        for n, (src, dst) in enumerate(((ids_hbm, ids_ref), (q_hbm, q_ref)))
    ]
    for copy in copies:
        copy.start()
    for copy in copies:
        copy.wait()
    for p in range(2):
        both = q_ref[p].astype(F32)
        for s in range(2):
            for h in range(16):
                kv, g = divmod(h, GROUP)
                row = kv * 32 + p * 16 + s * 8 + g
                rows_ref[row : row + 1, :] = both[s : s + 1, h * 128 : (h + 1) * 128]
    first, second = ids_ref[0].astype(F32), ids_ref[1].astype(F32)
    rows_ref[Q_ROWS:BLOCK_ROWS, :] = jnp.where(lanes((ID_ROWS, 128)) < 64, first, second)
    block = rows_ref[...].astype(BF16)
    for i in range(RING):
        out_ref[i] = block
    own_ref[...] = rows_ref[0:Q_ROWS, :]


def prefix_kernel(q_ref, own_ref, pair_ref, next_ref, cross_ref, local_ref, w_ref, out_ref):
    caches = (own_ref, pair_ref, next_ref, cross_ref)

    def table(kind, kv):
        cols = slice(kv * 128, (kv + 1) * 128)
        return jnp.concatenate(
            [jnp.concatenate([cache[g, kind, :, cols] for cache in caches], axis=0) for g in range(PROMPTS)],
            axis=1,
        )

    count = CHUNK * 32
    shape = (CHUNK, 32, 128)
    row_id = lax.broadcasted_iota(jnp.int32, shape, 1)
    lane_id = lanes(shape)
    spot = row_id + 32 * (lax.broadcasted_iota(jnp.int32, shape, 0) % 4)
    levels, dots, heads, bodies = [], [], [], []
    head_row = lax.broadcasted_iota(jnp.int32, (CHUNK, 8, 128), 1)
    facts = local_ref[0:8, :][None]
    for start in range(0, RING, CHUNK):
        block = q_ref[start : start + CHUNK].astype(F32)
        both = block[:, Q_ROWS:BLOCK_ROWS].reshape(CHUNK * ID_ROWS, 128)
        turned = pltpu.roll(both, 64, 1)
        left = lanes(both.shape) < 64
        ids = jnp.stack(
            [
                jnp.where(left, both, turned).reshape(CHUNK, 1, ID_ROWS, 128),
                jnp.where(left, turned, both).reshape(CHUNK, 1, ID_ROWS, 128),
            ],
            axis=1,
        )
        ids = jnp.broadcast_to(ids, (CHUNK, 2, 2, 8, 128)).reshape(count, 128)
        picks = [ids == float(g) for g in range(PROMPTS)]
        means, tops0, tops1, firsts = [], [], [], []
        for kv in range(2):
            q = block[:, kv * 32 : (kv + 1) * 32].reshape(count, 128)
            spread = jnp.concatenate([jnp.where(pick, q, 0.0).astype(BF16) for pick in picks], axis=1)
            scores = lax.dot_general(spread, table(0, kv), NT_DIMS, preferred_element_type=F32)
            top = jnp.max(scores, axis=1, keepdims=True)
            weights = jnp.exp2((scores - top) * FACTOR2)
            total = jnp.sum(weights, axis=1, keepdims=True)
            sums = jnp.dot(weights.astype(BF16), table(1, kv), preferred_element_type=F32)
            num = sums[:, 384:512]
            for g in (2, 1, 0):
                num = jnp.where(picks[g], sums[:, g * 128 : (g + 1) * 128], num)
            mean = (num / total).reshape(CHUNK, 2, 2, 8, 128)
            level = (top * FACTOR + jnp.log(total)).reshape(CHUNK, 2, 2, 8, 1)
            w = w_ref[kv * 8 : (kv + 1) * 8, :].reshape(1, 1, 8, 128)
            firsts.append(jnp.sum(mean[:, :, 0] * w, axis=-1, keepdims=True))
            tops0.append(level[:, :, 0])
            tops1.append(level[:, :, 1])
            means.append(mean[:, :, 1])

        def merge(pair):
            return jnp.stack(pair, axis=2).reshape(CHUNK, 32, pair[0].shape[-1])

        def pack(pair):
            wide = jnp.where(lane_id == spot, merge(pair), 0.0)
            return jnp.sum(wide.reshape(CHUNK // 4, 128, 128), axis=1)

        bodies.append(merge(means))
        levels.append(pack(tops0))
        dots.append(pack(firsts))
        high, mid, low = split(jnp.sum(jnp.where(lane_id == row_id, merge(tops1), 0.0), axis=1))
        line = high + pltpu.roll(mid, 32, 1) + pltpu.roll(low, 64, 1)
        head = jnp.where(head_row == 0, line[:, None, :], facts)
        heads.append(head)
    level, dot = jnp.concatenate(levels, axis=0), jnp.concatenate(dots, axis=0)
    my_level, my_dot = local_ref[8 : 8 + PLANE, :], local_ref[8 + PLANE : 8 + 2 * PLANE, :]
    top = jnp.maximum(level, my_level)
    old, new = jnp.exp(level - top), jnp.exp(my_level - top)
    dot = (dot * old + my_dot * new) / (old + new)
    level = top + jnp.log(old + new)
    for start, mean, head in zip(range(0, RING, CHUNK), bodies, heads):
        common = jnp.concatenate([*split(level), dot], axis=0)
        common = jnp.broadcast_to(common[None], (CHUNK, 4 * PLANE, 128))
        out_ref[start : start + CHUNK] = jnp.concatenate([mean, head, common], axis=1).astype(BF16)


def split(value):
    high = value.astype(BF16).astype(F32)
    rest = value - high
    mid = rest.astype(BF16).astype(F32)
    return high, mid, rest - mid


def local_attend(q, keys, values, fresh):
    q16 = q.astype(BF16)
    scores = lax.dot_general(q16, keys, NT_DIMS, preferred_element_type=F32)
    extra = [jnp.sum(q * k, axis=1, keepdims=True) for k, _ in fresh]
    top = jnp.max(scores, axis=1, keepdims=True)
    for e in extra:
        top = jnp.maximum(top, e)
    weights = jnp.exp2((scores - top) * FACTOR2)
    total = jnp.sum(weights, axis=1, keepdims=True)
    num = jnp.dot(weights.astype(BF16), values, preferred_element_type=F32)
    for e, (_, v) in zip(extra, fresh):
        weight = jnp.exp2((e - top) * FACTOR2)
        total = total + weight
        num = num + weight.astype(BF16).astype(F32) * v
    return num / total, top * FACTOR + jnp.log(total)


def first_kernel(
    ids_hbm, prior_hbm, q_hbm, kv_hbm, w_hbm, cache_hbm, out_ref, wide_hbm,
    ids_ref, prior_ref, q_ref, kv_ref, w_ref, wide_ref, sems, in_sems, out_sems,
):
    taken = [
        pltpu.make_async_copy(cache_hbm.at[p], wide_ref.at[p, :, 0:SUF, :], in_sems.at[p]) for p in range(2)
    ]
    given = [pltpu.make_async_copy(wide_ref.at[p], wide_hbm.at[p], out_sems.at[p]) for p in range(2)]
    pairs = ((kv_hbm, kv_ref), (q_hbm, q_ref), (w_hbm, w_ref), (ids_hbm, ids_ref), (prior_hbm, prior_ref))
    small = [pltpu.make_async_copy(src, dst, sems.at[n]) for n, (src, dst) in enumerate(pairs)]
    taken[0].start()
    for copy in small:
        copy.start()
    taken[1].start()
    for copy in small:
        copy.wait()
    queries = q_ref[...]
    step_kv = kv_ref[...].astype(F32)
    tail_row = lax.broadcasted_iota(jnp.int32, (TAIL, kv_ref.shape[-1]), 0)
    for p in range(2):
        for kind in range(2):
            line = step_kv[p, 0, kind : kind + 1, :]
            wide_ref[p, kind, SUF : SUF + TAIL, :] = jnp.where(tail_row == 0, line, 0.0).astype(BF16)
    for p in range(2):
        taken[p].wait()
        given[p].start()
    means, tops = [], []
    for p in range(2):
        for kv in range(2):
            cols = slice(kv * 128, (kv + 1) * 128)
            row = kv * 32 + p * 16
            mean, top = local_attend(
                queries[row : row + 8],
                wide_ref[p, 0, 0:SUF, cols],
                wide_ref[p, 1, 0:SUF, cols],
                [(step_kv[p, 0, 0:1, cols], step_kv[p, 0, 1:2, cols])],
            )
            means.append(mean)
            tops.append(top)
    w = w_ref[...]
    dot = jnp.sum(jnp.concatenate(means, axis=0) * jnp.concatenate([w, w], axis=0), axis=1, keepdims=True)
    top = jnp.concatenate(tops, axis=0)
    place = ring_place()
    spot = lax.broadcasted_iota(jnp.int32, (32, 128), 0) + 32 * (place % 4)
    lane_id = lanes((32, 128))
    level_row = jnp.sum(jnp.where(lane_id == spot, top, 0.0), axis=0, keepdims=True)
    dot_row = jnp.sum(jnp.where(lane_id == spot, dot, 0.0), axis=0, keepdims=True)
    here = lax.broadcasted_iota(jnp.int32, (PLANE, 128), 0) == place // 4
    here = here & (lanes((PLANE, 128)) // 32 == place % 4)
    out_ref[8 : 8 + PLANE, :] = jnp.where(here, level_row, -1e30)
    out_ref[8 + PLANE : 8 + 2 * PLANE, :] = jnp.where(here, dot_row, 0.0)
    slot = lanes((8, 128)) // 16 - (place % 4) * 2
    prior = jnp.where(slot == 0, prior_ref[0], jnp.where(slot == 1, prior_ref[1], 0.0))
    first, second = ids_ref[0].astype(F32), ids_ref[1].astype(F32)
    ids = jnp.where(slot == 0, first, jnp.where(slot == 1, second, 0.0))
    row_id = lax.broadcasted_iota(jnp.int32, (8, 128), 0)
    facts = jnp.where(row_id == 4, ids, 0.0)
    for r, part in enumerate(split(prior)):
        facts = jnp.where(row_id == r + 1, part, facts)
    out_ref[0:8, :] = facts
    for copy in given:
        copy.wait()


def second_kernel(
    anc_ref, q_ref, own_hbm, pair_hbm, far_hbm, kv_ref, copied_hbm, carried_ref, mean_ref, wide_ref, sems, out_sems
):
    core = lax.axis_index("core")
    base = 0
    for axis in DOM:
        base = base * 2 + lax.axis_index(axis)
    base = base * 2 - 2
    choices = []
    for slot in range(2):
        pos = anc_ref[slot] - base
        side, which = pos // 2, pos % 2
        from_own = side == 1
        from_pair = side == jnp.where(core == 0, 2, 0)
        from_far = side == jnp.where(core == 0, 0, 2)
        for j in range(2):
            for flag, cache in ((from_own, own_hbm), (from_pair, pair_hbm), (from_far, far_hbm)):
                copy = pltpu.make_async_copy(cache.at[j], wide_ref.at[slot], sems.at[slot])
                choices.append((flag & (which == j), copy))
    for flag, copy in choices:
        pl.when(flag)(copy.start)
    for flag, copy in choices:
        pl.when(flag)(copy.wait)
    results = [
        pltpu.make_async_copy(wide_ref.at[slot, :, 0:SUF, :], copied_hbm.at[slot], out_sems.at[slot])
        for slot in range(2)
    ]
    for slot in range(2):
        results[slot].start()
        for kind in range(2):
            tail = wide_ref[slot, kind, SUF : SUF + TAIL, :].astype(F32)
            carried_ref[slot, kind : kind + 1, :] = tail[0:1].astype(BF16)
    queries = q_ref[...]
    step_kv = kv_ref[...].astype(F32)
    carried = carried_ref[...].astype(F32)
    tops = []
    for p in range(2):
        for kv in range(2):
            cols = slice(kv * 128, (kv + 1) * 128)
            row = kv * 32 + p * 16 + 8
            mean, top = local_attend(
                queries[row : row + 8],
                wide_ref[p, 0, 0:SUF, cols],
                wide_ref[p, 1, 0:SUF, cols],
                [
                    (carried[p, 0:1, cols], carried[p, 1:2, cols]),
                    (step_kv[p, 1, 0:1, cols], step_kv[p, 1, 1:2, cols]),
                ],
            )
            mean_ref[p * 16 + kv * 8 : p * 16 + kv * 8 + 8, :] = mean
            tops.append(top)
    top = jnp.concatenate(tops, axis=0)
    row_id = lax.broadcasted_iota(jnp.int32, (32, 128), 0)
    row = jnp.sum(jnp.where(lanes((32, 128)) == row_id, top, 0.0), axis=0, keepdims=True)
    mean_ref[32:40, :] = jnp.broadcast_to(row, (8, 128))
    for result in results:
        result.wait()


def finish_kernel(part_ref, mean_ref, w_ref, out_ref, send_ref, wide_ref):
    parts = part_ref[...].astype(F32)
    heads = parts[:, OUT_ROWS : OUT_ROWS + 8]
    head_row = lax.broadcasted_iota(jnp.int32, heads.shape, 1)
    theirs = jnp.sum(jnp.where(head_row == 0, heads, 0.0), axis=1)
    theirs = theirs + pltpu.roll(theirs, 96, 1) + pltpu.roll(theirs, 64, 1)
    mine = mean_ref[32:33, :]
    top = jnp.maximum(jnp.max(theirs, axis=0, keepdims=True), mine)
    scale = jnp.exp(theirs - top)
    my_scale = jnp.exp(mine - top)
    inverse = 1.0 / (jnp.sum(scale, axis=0, keepdims=True) + my_scale)
    table = jnp.concatenate([scale * inverse, jnp.broadcast_to(my_scale * inverse, (128 - RING, 128))], axis=0).T
    attn = mean_ref[0:32, :] * table[0:32, RING : RING + 1]
    for i in range(RING):
        attn = attn + table[0:32, i : i + 1] * parts[i, 0:OUT_ROWS]
    w = w_ref[...]
    weighted = jnp.sum(attn * jnp.concatenate([w, w], axis=0), axis=1, keepdims=True)
    for p in range(2):
        for h in range(16):
            wide_ref[p : p + 1, h * 128 : (h + 1) * 128] = attn[p * 16 + h : p * 16 + h + 1, :]
    out_ref[...] = wide_ref[...].astype(BF16)

    base = OUT_ROWS + 8
    high, mid, low, dot = (parts[:, base + PLANE * t : base + PLANE * (t + 1)] for t in range(4))
    level = high + mid + low
    top = jnp.max(level, axis=0)
    scale = jnp.exp(level - top[None])
    twist = jnp.sum(scale * dot, axis=0) / jnp.sum(scale, axis=0)
    for shift in (8, 4, 2, 1):
        twist = twist + pltpu.roll(twist, 128 - shift, 1)
    facts = jnp.sum(heads.reshape(PLANE, 4, 8, 128), axis=1)
    fact_row = lax.broadcasted_iota(jnp.int32, facts.shape, 1)
    prior = jnp.sum(jnp.where((fact_row >= 1) & (fact_row <= 3), facts, 0.0), axis=1)
    ids = jnp.sum(jnp.where(fact_row == 4, facts, 0.0), axis=1)
    kind = lanes((PLANE, 128)) % 16
    line = jnp.where(kind == 0, twist, jnp.where(kind == 1, prior, jnp.where(kind == 2, ids, 0.0)))
    one = lanes((8 - PLANE, 128))
    second = jnp.zeros((8 - PLANE, 128), F32)
    for p in range(2):
        part = jnp.sum(weighted[p * 16 : (p + 1) * 16], axis=0, keepdims=True)
        second = jnp.where(one == p, part, second)
    block = jnp.concatenate([line, second], axis=0)
    for i in range(4 * NT):
        send_ref[i] = block


def weight_kernel(all_ref, log_ref, twist_ref):
    member = lax.axis_index("x0") * NC + lax.axis_index("core")
    place = ring_place()
    row_id = lax.broadcasted_iota(jnp.int32, (8, 128), 0)
    lane_id = lanes((8, 128))
    valid = (lane_id % 16 == 0) & (row_id < PLANE)
    raised, ids, values, twists = [], [], [], []
    own = jnp.zeros((8, 128), F32)
    own_ids = jnp.zeros((8, 128), F32)
    for m in range(4):
        rows = [all_ref[m * NT + t] for t in range(NT)]
        total = rows[0] + rows[1] + rows[2] + rows[3]
        total = jnp.where(row_id < PLANE, total + pltpu.roll(rows[0], 127, 1), total)
        own = jnp.where(member == m, total, own)
        raised.append(total)
        ids.append(pltpu.roll(rows[0], 126, 1))
        own_ids = jnp.where(member == m, ids[-1], own_ids)
    for p in range(2):
        here = (row_id == place // 4) & (lane_id == (place % 4) * 32 + p * 16)
        me = jnp.sum(jnp.where(here, own_ids, 0.0), keepdims=True)
        members = [valid & (i == me) for i in ids]
        masked = [jnp.where(m, r, -1e30) for m, r in zip(members, raised)]
        top = jnp.maximum(jnp.maximum(masked[0], masked[1]), jnp.maximum(masked[2], masked[3]))
        top = jnp.max(top, keepdims=True)
        shares = [jnp.where(m, jnp.exp(r - top), 0.0) for m, r in zip(members, raised)]
        amount = jnp.sum(shares[0] + shares[1] + shares[2] + shares[3], keepdims=True)
        mine = jnp.sum(jnp.where(here, own, 0.0), keepdims=True)
        value = mine - (jnp.log(amount) + top)
        values.append(value)
        twist = jnp.sum(jnp.where((row_id == PLANE) & (lane_id == p), own, 0.0), keepdims=True)
        twists.append(twist)
    one = lanes((1, 128))
    log_ref[...] = jnp.where(one == 0, values[0], values[1])[:, 0:2]
    twist_ref[...] = jnp.where(one == 0, twists[0], twists[1])[:, 0:2]


def body(
    prefix_cache, suffix_cache, queries, step_kv, twist_weight, prior_weights, prompt_ids, ancestors
):
    swap = [(0, 1), (1, 0)]
    cross = [(i, i + 1) for i in range(1, NZ * NX * NC - 1, 2)]
    cross = cross + [(b, a) for a, b in cross]
    next_prefix = lax.ppermute(prefix_cache, "x0", swap)
    pair_prefix = lax.ppermute(prefix_cache, "core", swap)
    weight_rows = twist_weight.reshape(16, 128)

    blocks, rows = pl.pallas_call(
        prep_kernel,
        out_shape=(
            jax.ShapeDtypeStruct((RING, BLOCK_ROWS, 128), BF16),
            jax.ShapeDtypeStruct((Q_ROWS, 128), F32),
        ),
        in_specs=[HBM] * 2,
        out_specs=(VMEM, VMEM),
        scratch_shapes=[
            pltpu.SMEM((2,), jnp.int32),
            pltpu.VMEM(queries.shape, BF16),
            pltpu.VMEM((BLOCK_ROWS, 128), F32),
            pltpu.SemaphoreType.DMA((2,)),
        ],
        compiler_params=WHOLE,
        name="prep",
    )(prompt_ids, queries)
    gathered = lax.all_to_all(blocks, PEERS, 0, 0, tiled=True)
    late_cache = lax.optimization_barrier((suffix_cache, blocks))[0]
    local, wide_cache = pl.pallas_call(
        first_kernel,
        out_shape=(
            jax.ShapeDtypeStruct((8 + 2 * PLANE, 128), F32),
            jax.ShapeDtypeStruct((2, 2, SUF + TAIL, 256), BF16),
        ),
        in_specs=[HBM] * 6,
        out_specs=(VMEM, HBM),
        scratch_shapes=[
            pltpu.SMEM((2,), jnp.int32),
            pltpu.SMEM((2,), F32),
            pltpu.VMEM((Q_ROWS, 128), F32),
            pltpu.VMEM(step_kv.shape, BF16),
            pltpu.VMEM((16, 128), F32),
            pltpu.VMEM((2, 2, SUF + TAIL, 256), BF16),
            pltpu.SemaphoreType.DMA((5,)),
            pltpu.SemaphoreType.DMA((2,)),
            pltpu.SemaphoreType.DMA((2,)),
        ],
        compiler_params=WHOLE,
        cost_estimate=LONG,
        name="first_local",
    )(prompt_ids, prior_weights, rows, step_kv, weight_rows, late_cache)
    held = lax.optimization_barrier((wide_cache, blocks))[0]
    after = lax.optimization_barrier((next_prefix, local))[0]
    cross_prefix = lax.ppermute(after, "core", swap)
    pair_cache = lax.ppermute(held, "core", swap)
    far_cache = lax.ppermute(held, DOM, cross)
    local = jnp.maximum(local, -3e38)
    parts = pl.pallas_call(
        prefix_kernel,
        out_shape=jax.ShapeDtypeStruct((RING, PART_ROWS, 128), BF16),
        in_specs=[VMEM] * 7,
        out_specs=VMEM,
        compiler_params=PARAMS,
        cost_estimate=LONG,
        name="prefix",
    )(
        gathered, prefix_cache, pair_prefix, next_prefix, cross_prefix, local, weight_rows
    )
    received = lax.all_to_all(parts, PEERS, 0, 0, tiled=True)
    copied, carried, mean = pl.pallas_call(
        second_kernel,
        out_shape=(
            jax.ShapeDtypeStruct(suffix_cache.shape, BF16),
            jax.ShapeDtypeStruct((2, 2, 256), BF16),
            jax.ShapeDtypeStruct((40, 128), F32),
        ),
        in_specs=[SMEM, VMEM] + [HBM] * 3 + [VMEM],
        out_specs=(HBM, VMEM, VMEM),
        scratch_shapes=[
            pltpu.VMEM((2, 2, SUF + TAIL, 256), BF16),
            pltpu.SemaphoreType.DMA((2,)),
            pltpu.SemaphoreType.DMA((2,)),
        ],
        compiler_params=MOST,
        name="second_local",
    )(ancestors, rows, wide_cache, pair_cache, far_cache, step_kv)
    attn, send = pl.pallas_call(
        finish_kernel,
        out_shape=(
            jax.ShapeDtypeStruct((2, 2048), BF16),
            jax.ShapeDtypeStruct((4 * NT, 8, 128), F32),
        ),
        in_specs=[VMEM] * 3,
        out_specs=(VMEM,) * 2,
        scratch_shapes=[pltpu.VMEM((2, 2048), F32)],
        compiler_params=PARAMS,
        name="finish",
    )(received, mean, weight_rows)
    lines = lax.all_to_all(send, SHARE + ("tp",), 0, 0, tiled=True)
    log_weights, twist_two = pl.pallas_call(
        weight_kernel,
        out_shape=(jax.ShapeDtypeStruct((1, 2), F32), jax.ShapeDtypeStruct((1, 2), F32)),
        in_specs=[VMEM],
        out_specs=(VMEM, VMEM),
        compiler_params=PARAMS,
        name="weights",
    )(lines)
    return (log_weights.reshape(2), copied, carried, attn, twist_two.reshape(2))


def solution(mesh):
    inner = Mesh(mesh.devices.reshape(2, 2, 2, 2, 2, NC, NT), WIDE)
    placed = (
        P(None, None, DOM, "tp"),
        P(DOM, None, None, "tp"),
        P(DOM, None, "tp"),
        P(DOM, None, None, "tp"),
        P("tp"),
        P(DOM),
        P(DOM),
        P(DOM),
    )
    return jax.shard_map(
        body,
        mesh=inner,
        in_specs=placed,
        out_specs=(
            P(DOM),
            P(DOM, None, None, "tp"),
            P(DOM, None, "tp"),
            P(DOM, "tp"),
            P(DOM),
        ),
        check_vma=False,
    )
```
